1024 devices in a mesh: blk: 32 (over z_lo, y), owner: 32 (over z_hi, x, core).
Axes of the slice: x: 4, y: 8, z: 16 (z_hi: 4, z_lo: 4; z = z_hi * 4 + z_lo), core: 2. Of those that a mesh axis runs over, the one named last changes fastest.
Arguments:
- amplitudes: bfloat16 [64, 32, 32768], P('owner', None, 'blk'), may hold values from -6 to 6
- integrals: bfloat16 [32, 1024, 1024], P('owner', 'blk'), may hold values from -0.1875 to 0.1875
- cd_tiles: int32 [32, 32], replicated, may hold values from 0 to 63, as said below
- cd_count: int32 [32], replicated, may hold values from 16 to 32, as said below
- ab_tiles: int32 [32, 32], replicated, may hold values from 0 to 63, as said below
- ab_count: int32 [32], replicated, may hold values from 16 to 32, as said below
Outputs:
- residual: float32 [64, 32, 32768], P('owner', None, 'blk')
The draws below stay inside these ranges and needn't reach their ends.
Inputs may be any that keep to these rules, and one draw needn't show every extreme that they name: `cd_tiles`: tile t is held by owner t // 2. The entries of one task's list are distinct, and at most 1 of them lie with one owner; only the first cd_count entries are used. `cd_count`: some task has 32 live entries. `ab_tiles`: tile t is held by owner t // 2. The entries of one task's list are distinct, and at most 1 of them lie with one owner; only the first ab_count entries are used. `ab_count`: some task has 32 live entries.
All inputs are finite; a program needn't handle non-finite values.
Results may differ from the reference program's by a relative error of at most 0.0029.
Values may be sent and summed in bfloat16 or wider, within the bound.
No kernel may reach another device: no remote copies, remote signals or barrier semaphores. Data moves between devices by JAX's collectives and lax.ppermute only.
A program may use at most 32 MiB of HBM per device.

```python
import jax
import jax.numpy as jnp
from jax import lax

TP = 32
TILE_DEV = 2
MAXT = 32
TASKS = 32
NTILES = 64
OPAIRS = 32768


def tile_lists(key):
    owners = NTILES // TILE_DEV
    task_keys = jax.random.split(key, TASKS)
    orders = jax.vmap(lambda single: jax.random.permutation(single, owners))(task_keys)
    offsets = jax.random.randint(jax.random.fold_in(key, 7), (TASKS, owners), 0, TILE_DEV)
    positions = jnp.arange(MAXT, dtype=jnp.int32)
    owner_of = orders[:, positions % owners]
    local = (jnp.take_along_axis(offsets, owner_of, axis=1) + positions[None, :] // owners) % TILE_DEV
    return (owner_of * TILE_DEV + local).astype(jnp.int32)


def live_counts(key):
    counts = jax.random.randint(jax.random.fold_in(key, 1), (TASKS,), (MAXT + 1) // 2, MAXT + 1)
    fullest = jax.random.randint(jax.random.fold_in(key, 2), (), 0, TASKS)
    return counts.at[fullest].set(MAXT).astype(jnp.int32)


def draw_cd_tiles(key, part):
    key = jax.random.fold_in(key, 11)
    return tile_lists(key)


def draw_cd_count(key, part):
    key = jax.random.fold_in(key, 12)
    return live_counts(key)


def draw_ab_tiles(key, part):
    key = jax.random.fold_in(key, 13)
    return tile_lists(key)


def draw_ab_count(key, part):
    key = jax.random.fold_in(key, 14)
    return live_counts(key)


def shard_levels(own_key, dims, shards, least, top_value):
    factor_of = 1.0
    for position, blocks in shards:
        heights = jax.random.uniform(jax.random.fold_in(jax.random.fold_in(own_key, 6), position), (blocks,), jnp.float32, least / len(shards), top_value / len(shards))
        factor_of = factor_of * jnp.repeat(jnp.exp(heights), dims[position] // blocks).reshape((-1,) + (1,) * (len(dims) - 1 - position))
    return factor_of


def bell_draw(own_key, extent, spread, limit, pieces=(), kind=jnp.bfloat16):
    factor_of = shard_levels(own_key, extent, pieces, -0.22, 0.18) if pieces else 1.0
    values = jax.random.normal(own_key, extent, jnp.float32) * spread * factor_of
    return jnp.minimum(jnp.maximum(values, -limit), limit).astype(kind)


def setup_inputs(seed: int = 0) -> dict:
    streams_of = jax.random.split(jax.random.key(seed), 7)
    amplitudes = bell_draw(streams_of[0], (NTILES, TP, OPAIRS), 1.0, 6.0, ((0, 32), (2, 32)))
    integrals = bell_draw(streams_of[1], (TASKS, MAXT * TP, MAXT * TP), (MAXT * TP) ** -0.5, 0.1875, ((0, 32), (1, 32)))
    cd_tiles = draw_cd_tiles(jax.random.fold_in(streams_of[6], 71), 0)
    cd_count = draw_cd_count(jax.random.fold_in(streams_of[6], 71), 0)
    ab_tiles = draw_ab_tiles(jax.random.fold_in(streams_of[6], 71), 0)
    ab_count = draw_ab_count(jax.random.fold_in(streams_of[6], 71), 0)
    return dict(amplitudes=amplitudes, integrals=integrals, cd_tiles=cd_tiles, cd_count=cd_count, ab_tiles=ab_tiles, ab_count=ab_count)


def reference(amplitudes, integrals, cd_tiles, cd_count, ab_tiles, ab_count):
    positions = jnp.arange(MAXT, dtype=jnp.int32)

    def one_task(task, residual):
        cd_row = lax.dynamic_index_in_dim(cd_tiles, task, 0, keepdims=False)
        ab_row = lax.dynamic_index_in_dim(ab_tiles, task, 0, keepdims=False)
        cd_live = (positions < lax.dynamic_index_in_dim(cd_count, task, 0, keepdims=False)).astype(amplitudes.dtype)
        ab_live = (positions < lax.dynamic_index_in_dim(ab_count, task, 0, keepdims=False)).astype(jnp.float32)
        block = jnp.take(amplitudes, cd_row, axis=0) * cd_live[:, None, None]
        stacked = block.reshape(MAXT * TP, OPAIRS)
        weights = lax.dynamic_index_in_dim(integrals, task, 0, keepdims=False)
        partial_sum = jnp.dot(weights, stacked, preferred_element_type=jnp.float32)
        rounded = lax.optimization_barrier(partial_sum.astype(jnp.bfloat16))
        partial_sum = rounded.astype(jnp.float32).reshape(MAXT, TP, OPAIRS) * ab_live[:, None, None]
        return residual.at[ab_row].add(partial_sum)

    start = jnp.zeros((NTILES, TP, OPAIRS), jnp.float32)
    return lax.fori_loop(0, TASKS, one_task, start)
```

```python
import jax
import jax.numpy as jnp
from jax import lax
from jax.sharding import PartitionSpec as P


def shards(amplitudes, integrals, cd_tiles, cd_count, ab_tiles, ab_count):
    tile_dev, width, occ = amplitudes.shape
    owners = lax.axis_size("owner")
    own = lax.axis_index("owner")
    tasks, list_len = cd_tiles.shape
    tiles = owners * tile_dev
    positions = jnp.arange(list_len, dtype=jnp.int32)

    gathered = lax.all_gather(amplitudes, "owner", axis=0, tiled=True)

    rows = lax.all_to_all(
        integrals[0].reshape(width, list_len, width),
        "blk", split_axis=0, concat_axis=0, tiled=True,
    )
    my_ab = lax.dynamic_index_in_dim(ab_tiles, own, 0, keepdims=False)
    my_ab_live = positions < lax.dynamic_index_in_dim(ab_count, own, 0, keepdims=False)
    route = (
        (jnp.arange(owners, dtype=jnp.int32)[:, None] == (my_ab // tile_dev)[None, :])
        & my_ab_live[None, :]
    ).astype(jnp.bfloat16)
    outgoing = jnp.einsum(
        "ok,kpc->opc", route, rows, preferred_element_type=jnp.float32
    ).astype(jnp.bfloat16)
    arrived = lax.all_to_all(outgoing, "owner", split_axis=0, concat_axis=0, tiled=True)
    ab_live = positions[None, :] < ab_count[:, None]
    local_idx = jnp.arange(tile_dev, dtype=jnp.int32)
    put_ab = jnp.sum(
        (
            (ab_tiles[None] == (own * tile_dev + local_idx)[:, None, None]) & ab_live[None]
        ).astype(jnp.float32),
        axis=2,
    )
    cd_live = positions[None, :] < cd_count[:, None]
    put_cd = (
        (jnp.arange(tiles, dtype=jnp.int32)[:, None, None] == cd_tiles[None]) & cd_live[None]
    ).astype(jnp.float32)
    place = (put_ab[:, None, :, None] * put_cd[None]).astype(jnp.bfloat16)
    summed = jnp.einsum("luqp,qpc->luc", place, arrived, preferred_element_type=jnp.float32)
    high = summed.astype(jnp.bfloat16)
    low = (summed - high.astype(jnp.float32)).astype(jnp.bfloat16)
    both = jnp.stack([high, low]).reshape(2 * tile_dev, tiles * width)
    weights = lax.all_gather(both, "blk", axis=0, tiled=False)
    weights = jnp.transpose(weights, (1, 0, 2)).reshape(2 * tile_dev * width, tiles * width)
    out = jnp.dot(
        weights, gathered.reshape(tiles * width, occ), preferred_element_type=jnp.float32
    ).reshape(2, tile_dev, width, occ)
    return out[0] + out[1]


def solution(mesh):
    placed = (P("owner", None, "blk"), P("owner", "blk", None), P(), P(), P(), P())
    return jax.shard_map(
        shards, mesh=mesh, in_specs=placed, out_specs=P("owner", None, "blk"), check_vma=False
    )
```

```python
import functools

import jax
import jax.numpy as jnp
from jax import lax
from jax.experimental import pallas as pl
from jax.experimental.pallas import tpu as pltpu
from jax.sharding import PartitionSpec as P

NZ, NX, NC = 4, 4, 2
SUB, LANE = 8, 128
SMEM = pl.BlockSpec(memory_space=pltpu.SMEM)
VMEM = pl.BlockSpec(memory_space=pltpu.VMEM)


def owner_index(z, x, core):
    return (z * NX + x) * NC + core


def lane_group(shape, width):
    return lax.broadcasted_iota(jnp.int32, shape, len(shape) - 1) // width


def order_columns(tiles_ref, count_ref, rows_ref, out_ref, total):
    own = lax.axis_index("owner")
    width, columns = rows_ref.shape
    list_len = tiles_ref.shape[1]
    groups = LANE // width
    total[...] = jnp.zeros_like(total)
    count = count_ref[own]
    group = lane_group((width, LANE), width)
    for place in range(list_len):
        if place % groups == 0:
            chunk = rows_ref[:, place // groups * LANE : (place // groups + 1) * LANE].astype(jnp.float32)
        owner = tiles_ref[own, place] // 2
        spot = (owner // NC) % NX
        target = owner // (NX * NC) * NC + owner % NC
        turned = pltpu.roll(chunk, (spot - place % groups + groups) % groups * width, 1)
        keep = (group == spot) & (place < count)
        total[target] += jnp.where(keep, turned, 0.0)
    for part in range(width // SUB):
        for target in range(NZ * NC):
            out_ref[part, target] = total[target, part * SUB : (part + 1) * SUB, :].astype(out_ref.dtype)


def regroup(tiles, width):
    count = len(tiles)
    group = lane_group(tiles[0].shape, width)
    results = []
    for i in range(count):
        merged = None
        for j in range(count):
            shift = (j - i) % count * width
            turned = pltpu.roll(tiles[j], shift, tiles[j].ndim - 1) if shift else tiles[j]
            merged = turned if merged is None else jnp.where(group == j, turned, merged)
        results.append(merged)
    return results


def route(tiles_ref, count_ref, rows_ref, out_ref, held):
    own = lax.axis_index("owner")
    list_len = tiles_ref.shape[1]
    held[...] = jnp.zeros_like(held)
    count = count_ref[own]
    for place in range(list_len):
        owner = tiles_ref[own, place] // 2
        held[owner] += jnp.where(place < count, rows_ref[place].astype(jnp.float32), 0.0)
    for z in range(NZ):
        for core in range(NC):
            moved = regroup([held[owner_index(z, x, core)] for x in range(NX)], LANE // NX)
            for x in range(NX):
                out_ref[owner_index(z, x, core)] = moved[x].astype(out_ref.dtype)


def accumulate(ab_ref, ab_count_ref, cd_ref, cd_count_ref, rows_ref, out_ref, mask):
    own, piece = lax.axis_index("owner"), lax.axis_index("blk")
    chunk = piece % (NZ * NC)
    z, x, core = own // (NX * NC), (own // NC) % NX, own % NC
    tasks, list_len = ab_ref.shape
    place = lax.broadcasted_iota(jnp.int32, (tasks, list_len), 1)
    ab_list = jnp.where(place < ab_count_ref[...], ab_ref[...], -1)
    cd_list = jnp.where(place < cd_count_ref[...], cd_ref[...], -1)
    cd_owner = owner_index(chunk // NC, x, chunk % NC)
    group = lane_group((tasks, LANE), LANE // NX)
    cd_hit = [
        jnp.max((cd_list == cd_owner * 2 + par).astype(jnp.float32), axis=1, keepdims=True) for par in range(2)
    ]
    for low in range(2):
        ab_hit = jnp.zeros((tasks, LANE), jnp.float32)
        for spot in range(NX):
            tile = owner_index(z, spot, core) * 2 + low
            hit = jnp.max((ab_list == tile).astype(jnp.float32), axis=1, keepdims=True)
            ab_hit = jnp.where(group == spot, hit, ab_hit)
        for par in range(2):
            mask[low * 2 + par] = ab_hit * cd_hit[par]
    totals = [jnp.zeros((SUB, LANE), jnp.float32) for _ in range(4)]
    for task in range(tasks):
        rows = rows_ref[task].astype(jnp.float32)
        for kind in range(4):
            totals[kind] += rows * mask[kind, task : task + 1, :]
    for kind in range(4):
        rounded = totals[kind].astype(out_ref.dtype)
        for target in range(out_ref.shape[0]):
            out_ref[target, kind] = rounded


def multiply(weights_ref, amps_ref, out_ref, left):
    width = amps_ref.shape[2]
    chunks = NZ * NC
    groups = LANE // width
    half = chunks // groups
    for kind in range(4):
        low, par = kind // 2, kind % 2
        for side in range(half):
            parts = []
            for part in range(width // SUB):
                tiles = [
                    weights_ref[part * chunks + side * groups + j, kind].astype(jnp.float32) for j in range(groups)
                ]
                parts.append(regroup(tiles, width))
            for spot in range(NX):
                rows = jnp.concatenate([p[spot] for p in parts], axis=0)
                row, col = (spot * 2 + low) * width, (par * half + side) * LANE
                left[row : row + width, col : col + LANE] = rows.astype(left.dtype)
    deep = chunks * width
    occ = amps_ref.shape[3]
    step = 256
    for col in range(0, occ, step):
        total = None
        for par in range(2):
            right = amps_ref[:, par, :, col : col + step].reshape(deep, step)
            term = jnp.dot(left[:, par * deep : (par + 1) * deep], right, preferred_element_type=jnp.float32)
            total = term if total is None else total + term
        out_ref[:, :, col : col + step] = total.reshape(NX, 2 * width, step).astype(out_ref.dtype)


def shards(amplitudes, integrals, cd_tiles, cd_count, ab_tiles, ab_count):
    tile_dev, width, occ = amplitudes.shape
    owners, pieces = lax.axis_size("owner"), lax.axis_size("blk")
    tasks = cd_tiles.shape[0]
    side_groups = [[owner_index(z, x, core) for z in range(NZ) for core in range(NC)] for x in range(NX)]
    x_groups = [[owner_index(z, x, core) for x in range(NX)] for z in range(NZ) for core in range(NC)]
    bf16, f32 = jnp.bfloat16, jnp.float32

    gathered = lax.all_gather(amplitudes, "owner", axis=0, tiled=True, axis_index_groups=side_groups)
    gathered = gathered.reshape(NZ * NC, tile_dev, width, occ)

    ordered = pl.pallas_call(
        order_columns,
        out_shape=jax.ShapeDtypeStruct((width // SUB, NZ * NC, SUB, LANE), bf16),
        in_specs=[SMEM, SMEM, VMEM],
        out_specs=VMEM,
        scratch_shapes=[pltpu.VMEM((NZ * NC, width, LANE), f32)],
        name="order_columns",
    )(cd_tiles, cd_count, integrals[0])
    ordered = ordered.reshape(pieces, SUB, LANE)
    mine = lax.all_to_all(ordered, "blk", split_axis=0, concat_axis=0, tiled=True)
    outgoing = pl.pallas_call(
        route,
        out_shape=jax.ShapeDtypeStruct((owners, SUB, LANE), bf16),
        in_specs=[SMEM, SMEM, VMEM],
        out_specs=VMEM,
        scratch_shapes=[pltpu.VMEM((owners, SUB, LANE), f32)],
        name="route",
    )(ab_tiles, ab_count, mine)
    arrived = lax.all_to_all(outgoing, "owner", split_axis=0, concat_axis=0, tiled=True)
    spread = pl.pallas_call(
        accumulate,
        out_shape=jax.ShapeDtypeStruct((pieces, 4, SUB, LANE), bf16),
        in_specs=[VMEM] * 5,
        out_specs=VMEM,
        scratch_shapes=[pltpu.VMEM((4, tasks, LANE), f32)],
        name="accumulate",
    )(ab_tiles, ab_count[:, None], cd_tiles, cd_count[:, None], arrived)
    weights = lax.all_to_all(spread, "blk", split_axis=0, concat_axis=0, tiled=True)
    partial = pl.pallas_call(
        multiply,
        out_shape=jax.ShapeDtypeStruct((NX, tile_dev * width, occ), f32),
        in_specs=[VMEM, VMEM],
        out_specs=VMEM,
        scratch_shapes=[pltpu.VMEM((NX * tile_dev * width, NZ * NC * tile_dev * width), bf16)],
        compiler_params=pltpu.CompilerParams(vmem_limit_bytes=32 * 1024 * 1024),
        name="multiply",
    )(weights, gathered)
    parts = lax.all_to_all(
        partial, "owner", split_axis=0, concat_axis=0, tiled=True, axis_index_groups=x_groups
    )
    return jnp.sum(parts, axis=0).reshape(tile_dev, width, occ)


def solution(mesh):
    placed = (P("owner", None, "blk"), P("owner", "blk", None), P(), P(), P(), P())
    return jax.shard_map(
        shards, mesh=mesh, in_specs=placed, out_specs=P("owner", None, "blk"), check_vma=False
    )
```

```python
import functools

import jax
import jax.numpy as jnp
from jax import lax
from jax.experimental import pallas as pl
from jax.experimental.pallas import tpu as pltpu
from jax.sharding import PartitionSpec as P

NZ, NX, NC = 4, 4, 2
SUB, LANE = 8, 128
SMEM = pl.BlockSpec(memory_space=pltpu.SMEM)
VMEM = pl.BlockSpec(memory_space=pltpu.VMEM)
ANY = pl.BlockSpec(memory_space=pl.ANY)
STEPS = (0, -1, 1, 2)


def owner_index(z, x, core):
    return (z * NX + x) * NC + core


def lane_group(shape, width):
    return lax.broadcasted_iota(jnp.int32, shape, len(shape) - 1) // width


def order_columns(tiles_ref, count_ref, rows_ref, out_ref, total):
    own = lax.axis_index("owner")
    width, columns = rows_ref.shape
    list_len = tiles_ref.shape[1]
    groups = LANE // width
    total[...] = jnp.zeros_like(total)
    count = count_ref[own]
    group = lane_group((width, LANE), width)
    for place in range(list_len):
        if place % groups == 0:
            chunk = rows_ref[:, place // groups * LANE : (place // groups + 1) * LANE].astype(jnp.float32)
        owner = tiles_ref[own, place] // 2
        spot = (owner // NC) % NX
        target = owner // (NX * NC) * NC + owner % NC
        turned = pltpu.roll(chunk, (spot - place % groups + groups) % groups * width, 1)
        keep = (group == spot) & (place < count)
        total[target] += jnp.where(keep, turned, 0.0)
    for part in range(width // SUB):
        for target in range(NZ * NC):
            out_ref[part, target] = total[target, part * SUB : (part + 1) * SUB, :].astype(out_ref.dtype)


def regroup(tiles, width):
    count = len(tiles)
    group = lane_group(tiles[0].shape, width)
    results = []
    for i in range(count):
        merged = None
        for j in range(count):
            shift = (j - i) % count * width
            turned = pltpu.roll(tiles[j], shift, tiles[j].ndim - 1) if shift else tiles[j]
            merged = turned if merged is None else jnp.where(group == j, turned, merged)
        results.append(merged)
    return results


def route(tiles_ref, count_ref, rows_ref, *rest):
    out_ref, held = rest[-2:]
    own = lax.axis_index("owner")
    list_len = tiles_ref.shape[1]
    held[...] = jnp.zeros_like(held)
    count = count_ref[own]
    for place in range(list_len):
        owner = tiles_ref[own, place] // 2
        held[owner] += jnp.where(place < count, rows_ref[place].astype(jnp.float32), 0.0)
    for z in range(NZ):
        for core in range(NC):
            moved = regroup([held[owner_index(z, x, core)] for x in range(NX)], LANE // NX)
            for x in range(NX):
                out_ref[owner_index(z, x, core)] = moved[x].astype(out_ref.dtype)


def accumulate(ab_ref, ab_count_ref, cd_ref, cd_count_ref, rows_ref, *rest):
    out_ref, mask = rest[-2:]
    own, piece = lax.axis_index("owner"), lax.axis_index("blk")
    chunk = piece % (NZ * NC)
    z, x, core = own // (NX * NC), (own // NC) % NX, own % NC
    tasks, list_len = ab_ref.shape
    place = lax.broadcasted_iota(jnp.int32, (tasks, list_len), 1)
    ab_list = jnp.where(place < ab_count_ref[...], ab_ref[...], -1)
    cd_list = jnp.where(place < cd_count_ref[...], cd_ref[...], -1)
    cd_owner = owner_index(chunk // NC, x, chunk % NC)
    group = lane_group((tasks, LANE), LANE // NX)
    cd_hit = [
        jnp.max((cd_list == cd_owner * 2 + par).astype(jnp.float32), axis=1, keepdims=True) for par in range(2)
    ]
    for low in range(2):
        ab_hit = jnp.zeros((tasks, LANE), jnp.float32)
        for spot in range(NX):
            tile = owner_index(z, spot, core) * 2 + low
            hit = jnp.max((ab_list == tile).astype(jnp.float32), axis=1, keepdims=True)
            ab_hit = jnp.where(group == spot, hit, ab_hit)
        for par in range(2):
            mask[low * 2 + par] = ab_hit * cd_hit[par]
    totals = [jnp.zeros((SUB, LANE), jnp.float32) for _ in range(4)]
    for task in range(tasks):
        rows = rows_ref[task].astype(jnp.float32)
        for kind in range(4):
            totals[kind] += rows * mask[kind, task : task + 1, :]
    for kind in range(4):
        rounded = totals[kind].astype(out_ref.dtype)
        for target in range(out_ref.shape[0]):
            out_ref[target, kind] = rounded


def multiply(weights_ref, own_ref, other_ref, out_ref, left):
    own = lax.axis_index("owner")
    z, core = own // (NX * NC), own % NC
    width, occ = own_ref.shape[2:]
    chunks = NZ * NC
    for kind in range(4):
        low, par = kind // 2, kind % 2
        for side in range(NC):
            parts = []
            for part in range(width // SUB):
                tiles = []
                for step in STEPS:
                    chunk = (z + step + NZ) % NZ * NC + (core + side) % NC
                    tiles.append(weights_ref[part * chunks + chunk, kind].astype(jnp.float32))
                parts.append(regroup(tiles, width))
            for spot in range(NX):
                rows = jnp.concatenate([p[spot] for p in parts], axis=0)
                row, col = (spot * 2 + low) * width, (par * NC + side) * LANE
                left[row : row + width, col : col + LANE] = rows.astype(left.dtype)
    wide = 256
    for col in range(0, occ, wide):
        total = None
        for par in range(2):
            for side, amps in enumerate((own_ref, other_ref)):
                right = amps[:, par, :, col : col + wide].reshape(LANE, wide)
                at = (par * NC + side) * LANE
                term = jnp.dot(left[:, at : at + LANE], right, preferred_element_type=jnp.float32)
                total = term if total is None else total + term
        out_ref[:, :, col : col + wide] = total.reshape(NX, 2 * width, wide).astype(out_ref.dtype)


def moved(block, dz, dcore=0):
    pairs = [
        (owner_index(z, x, core), owner_index((z + dz) % NZ, x, (core + dcore) % NC))
        for z in range(NZ)
        for x in range(NX)
        for core in range(NC)
    ]
    return lax.ppermute(block, "owner", pairs)


def shards(amplitudes, integrals, cd_tiles, cd_count, ab_tiles, ab_count):
    tile_dev, width, occ = amplitudes.shape
    owners, pieces = lax.axis_size("owner"), lax.axis_size("blk")
    tasks = cd_tiles.shape[0]
    x_groups = [[owner_index(z, x, core) for x in range(NX)] for z in range(NZ) for core in range(NC)]
    bf16, f32 = jnp.bfloat16, jnp.float32

    ordered = pl.pallas_call(
        order_columns,
        out_shape=jax.ShapeDtypeStruct((width // SUB, NZ * NC, SUB, LANE), bf16),
        in_specs=[SMEM, SMEM, VMEM],
        out_specs=VMEM,
        scratch_shapes=[pltpu.VMEM((NZ * NC, width, LANE), f32)],
        name="order_columns",
    )(cd_tiles, cd_count, integrals[0])
    ordered = ordered.reshape(pieces, SUB, LANE)
    mine = lax.all_to_all(ordered, "blk", split_axis=0, concat_axis=0, tiled=True)
    below, above = moved(amplitudes, 1), moved(amplitudes, NZ - 1)
    outgoing = pl.pallas_call(
        route,
        out_shape=jax.ShapeDtypeStruct((owners, SUB, LANE), bf16),
        in_specs=[SMEM, SMEM, VMEM, ANY, ANY],
        out_specs=VMEM,
        scratch_shapes=[pltpu.VMEM((owners, SUB, LANE), f32)],
        name="route",
    )(ab_tiles, ab_count, mine, below, above)
    arrived = lax.all_to_all(outgoing, "owner", split_axis=0, concat_axis=0, tiled=True)
    far = (moved(above[:1], NZ - 1), moved(below[1:], 1))
    spread = pl.pallas_call(
        accumulate,
        out_shape=jax.ShapeDtypeStruct((pieces, 4, SUB, LANE), bf16),
        in_specs=[VMEM] * 5 + [ANY] * 2,
        out_specs=VMEM,
        scratch_shapes=[pltpu.VMEM((4, tasks, LANE), f32)],
        name="accumulate",
    )(ab_tiles, ab_count[:, None], cd_tiles, cd_count[:, None], arrived, *far)
    weights = lax.all_to_all(spread, "blk", split_axis=0, concat_axis=0, tiled=True)
    own_side = jnp.concatenate([amplitudes, below, above, *far], axis=0).reshape(NZ, tile_dev, width, occ)
    other_side = moved(own_side, 0, 1)
    partial = pl.pallas_call(
        multiply,
        out_shape=jax.ShapeDtypeStruct((NX, tile_dev * width, occ), f32),
        in_specs=[VMEM, VMEM, VMEM],
        out_specs=VMEM,
        scratch_shapes=[pltpu.VMEM((NX * tile_dev * width, NZ * NC * tile_dev * width), bf16)],
        compiler_params=pltpu.CompilerParams(vmem_limit_bytes=32 * 1024 * 1024),
        name="multiply",
    )(weights, own_side, other_side)
    parts = lax.all_to_all(
        partial, "owner", split_axis=0, concat_axis=0, tiled=True, axis_index_groups=x_groups
    )
    return jnp.sum(parts, axis=0).reshape(tile_dev, width, occ)


def solution(mesh):
    placed = (P("owner", None, "blk"), P("owner", "blk", None), P(), P(), P(), P())
    return jax.shard_map(
        shards, mesh=mesh, in_specs=placed, out_specs=P("owner", None, "blk"), check_vma=False
    )
```

```python
import functools

import jax
import jax.numpy as jnp
from jax import lax
from jax.experimental import pallas as pl
from jax.experimental.pallas import tpu as pltpu
from jax.sharding import PartitionSpec as P

NZ, NX, NC = 4, 4, 2
SUB, LANE = 8, 128
SMEM = pl.BlockSpec(memory_space=pltpu.SMEM)
VMEM = pl.BlockSpec(memory_space=pltpu.VMEM)
ANY = pl.BlockSpec(memory_space=pl.ANY)
SMALL = pltpu.CompilerParams(vmem_limit_bytes=4 * 1024 * 1024)
STEPS = (0, 1, 3, 2)


def owner_index(z, x, core):
    return (z * NX + x) * NC + core


def lane_group(shape, width):
    return lax.broadcasted_iota(jnp.int32, shape, len(shape) - 1) // width


def order_columns(tiles_ref, count_ref, rows_ref, out_ref, total):
    own = lax.axis_index("owner")
    width, columns = rows_ref.shape
    list_len = tiles_ref.shape[1]
    groups = LANE // width
    total[...] = jnp.zeros_like(total)
    count = count_ref[own]
    group = lane_group((width, LANE), width)
    for place in range(list_len):
        if place % groups == 0:
            chunk = rows_ref[:, place // groups * LANE : (place // groups + 1) * LANE].astype(jnp.float32)
        owner = tiles_ref[own, place] // 2
        spot = (owner // NC) % NX
        target = owner // (NX * NC) * NC + owner % NC
        turned = pltpu.roll(chunk, (spot - place % groups + groups) % groups * width, 1)
        keep = (group == spot) & (place < count)
        total[target] += jnp.where(keep, turned, 0.0)
    for part in range(width // SUB):
        for target in range(NZ * NC):
            out_ref[part, target] = total[target, part * SUB : (part + 1) * SUB, :].astype(out_ref.dtype)


def regroup(tiles, width):
    count = len(tiles)
    group = lane_group(tiles[0].shape, width)
    results = []
    for i in range(count):
        merged = None
        for j in range(count):
            shift = (j - i) % count * width
            turned = pltpu.roll(tiles[j], shift, tiles[j].ndim - 1) if shift else tiles[j]
            merged = turned if merged is None else jnp.where(group == j, turned, merged)
        results.append(merged)
    return results


def route(tiles_ref, count_ref, rows_ref, *rest):
    out_ref, held = rest[-2:]
    own = lax.axis_index("owner")
    list_len = tiles_ref.shape[1]
    held[...] = jnp.zeros_like(held)
    count = count_ref[own]
    for place in range(list_len):
        owner = tiles_ref[own, place] // 2
        held[owner] += jnp.where(place < count, rows_ref[place].astype(jnp.float32), 0.0)
    for z in range(NZ):
        for core in range(NC):
            moved = regroup([held[owner_index(z, x, core)] for x in range(NX)], LANE // NX)
            for x in range(NX):
                out_ref[owner_index(z, x, core)] = moved[x].astype(out_ref.dtype)


def accumulate(ab_ref, ab_count_ref, cd_ref, cd_count_ref, rows_ref, *rest):
    out_ref, mask = rest[-2:]
    own, piece = lax.axis_index("owner"), lax.axis_index("blk")
    chunk = piece % (NZ * NC)
    z, x, core = own // (NX * NC), (own // NC) % NX, own % NC
    tasks, list_len = ab_ref.shape
    place = lax.broadcasted_iota(jnp.int32, (tasks, list_len), 1)
    task = lax.broadcasted_iota(jnp.int32, (tasks, tasks), 0)
    same = task == lax.broadcasted_iota(jnp.int32, (tasks, tasks), 1)

    def live(list_ref, count_ref):
        counts = jnp.where(same, count_ref[...].astype(jnp.float32), 0.0)
        counts = jnp.sum(counts, axis=1, keepdims=True)
        return jnp.where(place.astype(jnp.float32) < counts, list_ref[...], -1)

    ab_list, cd_list = live(ab_ref, ab_count_ref), live(cd_ref, cd_count_ref)
    cd_owner = owner_index(chunk // NC, x, chunk % NC)
    group = lane_group((tasks, LANE), LANE // NX)
    cd_hit = [
        jnp.max((cd_list == cd_owner * 2 + par).astype(jnp.float32), axis=1, keepdims=True) for par in range(2)
    ]
    for low in range(2):
        ab_hit = jnp.zeros((tasks, LANE), jnp.float32)
        for spot in range(NX):
            tile = owner_index(z, spot, core) * 2 + low
            hit = jnp.max((ab_list == tile).astype(jnp.float32), axis=1, keepdims=True)
            ab_hit = jnp.where(group == spot, hit, ab_hit)
        for par in range(2):
            mask[low * 2 + par] = ab_hit * cd_hit[par]
    totals = [jnp.zeros((SUB, LANE), jnp.float32) for _ in range(4)]
    for task in range(tasks):
        rows = rows_ref[task].astype(jnp.float32)
        for kind in range(4):
            totals[kind] += rows * mask[kind, task : task + 1, :]
    for kind in range(4):
        rounded = totals[kind].astype(out_ref.dtype)
        for target in range(out_ref.shape[0]):
            out_ref[target, kind] = rounded


def settle(first_ref, second_ref, out_ref):
    pass


def collect(*refs):
    for place, ref in enumerate(refs[:-1]):
        refs[-1][place] = ref[...]


def multiply(weights_ref, own_ref, other_ref, out_ref, left):
    own = lax.axis_index("owner")
    z, core = own // (NX * NC), own % NC
    width, occ = own_ref.shape[2:]
    chunks = NZ * NC
    for kind in range(4):
        low, par = kind // 2, kind % 2
        for side in range(NC):
            parts = []
            for part in range(width // SUB):
                tiles = []
                for step in STEPS:
                    chunk = (z ^ step) * NC + (core + side) % NC
                    tiles.append(weights_ref[part * chunks + chunk, kind].astype(jnp.float32))
                parts.append(regroup(tiles, width))
            for spot in range(NX):
                rows = jnp.concatenate([p[spot] for p in parts], axis=0)
                row, col = (spot * 2 + low) * width, (par * NC + side) * LANE
                left[row : row + width, col : col + LANE] = rows.astype(left.dtype)
    wide = 256
    for col in range(0, occ, wide):
        total = None
        for par in range(2):
            for side, amps in enumerate((own_ref, other_ref)):
                right = amps[:, par, :, col : col + wide].reshape(LANE, wide)
                at = (par * NC + side) * LANE
                term = jnp.dot(left[:, at : at + LANE], right, preferred_element_type=jnp.float32)
                total = term if total is None else total + term
        out_ref[:, :, col : col + wide] = total.reshape(NX, 2 * width, wide).astype(out_ref.dtype)


def moved(block, dz, dcore=0):
    pairs = [
        (owner_index(z, x, core), owner_index(z ^ dz, x, core ^ dcore))
        for z in range(NZ)
        for x in range(NX)
        for core in range(NC)
    ]
    return lax.ppermute(block, "owner", pairs)


def shards(amplitudes, integrals, cd_tiles, cd_count, ab_tiles, ab_count):
    tile_dev, width, occ = amplitudes.shape
    owners, pieces = lax.axis_size("owner"), lax.axis_size("blk")
    tasks = cd_tiles.shape[0]
    x_groups = [[owner_index(z, x, core) for x in range(NX)] for z in range(NZ) for core in range(NC)]
    bf16, f32 = jnp.bfloat16, jnp.float32

    first, second = moved(amplitudes, 1), moved(amplitudes, 3)
    second = pl.pallas_call(
        settle,
        out_shape=jax.ShapeDtypeStruct(second.shape, second.dtype),
        in_specs=[ANY, ANY],
        out_specs=ANY,
        input_output_aliases={1: 0},
        cost_estimate=pl.CostEstimate(flops=10**10, bytes_accessed=second.size * 4, transcendentals=0),
        compiler_params=SMALL,
        name="settle",
    )(first, second)
    blocks = [amplitudes, first, second, moved(second, 1)]
    own_side = pl.pallas_call(
        collect,
        out_shape=jax.ShapeDtypeStruct((NZ, tile_dev, width, occ), bf16),
        in_specs=[VMEM] * NZ,
        out_specs=VMEM,
        cost_estimate=pl.CostEstimate(flops=10000000000, bytes_accessed=NZ * amplitudes.size * 4, transcendentals=0),
        compiler_params=SMALL,
        name="collect",
    )(*blocks)
    other_side = moved(own_side, 0, 1)

    ordered = pl.pallas_call(
        order_columns,
        out_shape=jax.ShapeDtypeStruct((width // SUB, NZ * NC, SUB, LANE), bf16),
        in_specs=[SMEM, SMEM, VMEM],
        out_specs=VMEM,
        scratch_shapes=[pltpu.VMEM((NZ * NC, width, LANE), f32)],
        name="order_columns",
    )(cd_tiles, cd_count, integrals[0])
    ordered = ordered.reshape(pieces, SUB, LANE)
    mine = lax.all_to_all(ordered, "blk", split_axis=0, concat_axis=0, tiled=True)
    outgoing = pl.pallas_call(
        route,
        out_shape=jax.ShapeDtypeStruct((owners, SUB, LANE), bf16),
        in_specs=[SMEM, SMEM, VMEM],
        out_specs=VMEM,
        scratch_shapes=[pltpu.VMEM((owners, SUB, LANE), f32)],
        compiler_params=SMALL,
        name="route",
    )(ab_tiles, ab_count, mine)
    arrived = lax.all_to_all(outgoing, "owner", split_axis=0, concat_axis=0, tiled=True)
    spread = pl.pallas_call(
        accumulate,
        out_shape=jax.ShapeDtypeStruct((pieces, 4, SUB, LANE), bf16),
        in_specs=[VMEM] * 5,
        out_specs=VMEM,
        scratch_shapes=[pltpu.VMEM((4, tasks, LANE), f32)],
        compiler_params=SMALL,
        name="accumulate",
    )(ab_tiles, ab_count[None, :], cd_tiles, cd_count[None, :], arrived)
    weights = lax.all_to_all(spread, "blk", split_axis=0, concat_axis=0, tiled=True)
    partial = pl.pallas_call(
        multiply,
        out_shape=jax.ShapeDtypeStruct((NX, tile_dev * width, occ), f32),
        in_specs=[VMEM, VMEM, VMEM],
        out_specs=VMEM,
        scratch_shapes=[pltpu.VMEM((NX * tile_dev * width, NZ * NC * tile_dev * width), bf16)],
        compiler_params=pltpu.CompilerParams(vmem_limit_bytes=16 * 1024 * 1024),
        name="multiply",
    )(weights, own_side, other_side)
    parts = lax.all_to_all(
        partial, "owner", split_axis=0, concat_axis=0, tiled=True, axis_index_groups=x_groups
    )
    return jnp.sum(parts, axis=0).reshape(tile_dev, width, occ)


def solution(mesh):
    placed = (P("owner", None, "blk"), P("owner", "blk", None), P(), P(), P(), P())
    return jax.shard_map(
        shards, mesh=mesh, in_specs=placed, out_specs=P("owner", None, "blk"), check_vma=False
    )
```

```python
import functools

import jax
import jax.numpy as jnp
from jax import lax
from jax.experimental import pallas as pl
from jax.experimental.pallas import tpu as pltpu
from jax.sharding import PartitionSpec as P

NZ, NX, NC = 4, 4, 2
SUB, LANE = 8, 128
SMEM = pl.BlockSpec(memory_space=pltpu.SMEM)
VMEM = pl.BlockSpec(memory_space=pltpu.VMEM)
ANY = pl.BlockSpec(memory_space=pl.ANY)
SMALL = pltpu.CompilerParams(vmem_limit_bytes=4 * 1024 * 1024)
STEPS = (0, 1, 3, 2)


def owner_index(z, x, core):
    return (z * NX + x) * NC + core


def lane_group(shape, width):
    return lax.broadcasted_iota(jnp.int32, shape, len(shape) - 1) // width


def order_columns(tiles_ref, count_ref, rows_ref, out_ref, total):
    own = lax.axis_index("owner")
    width, columns = rows_ref.shape
    list_len = tiles_ref.shape[1]
    groups = LANE // width
    total[...] = jnp.zeros_like(total)
    count = count_ref[own]
    group = lane_group((width, LANE), width)
    for place in range(list_len):
        if place % groups == 0:
            chunk = rows_ref[:, place // groups * LANE : (place // groups + 1) * LANE].astype(jnp.float32)
        owner = tiles_ref[own, place] // 2
        spot = (owner // NC) % NX
        target = owner // (NX * NC) * NC + owner % NC
        turned = pltpu.roll(chunk, (spot - place % groups + groups) % groups * width, 1)
        keep = (group == spot) & (place < count)
        total[target] += jnp.where(keep, turned, 0.0)
    for part in range(width // SUB):
        for target in range(NZ * NC):
            out_ref[part, target] = total[target, part * SUB : (part + 1) * SUB, :].astype(out_ref.dtype)


def regroup(tiles, width):
    count = len(tiles)
    group = lane_group(tiles[0].shape, width)
    results = []
    for i in range(count):
        merged = None
        for j in range(count):
            shift = (j - i) % count * width
            turned = pltpu.roll(tiles[j], shift, tiles[j].ndim - 1) if shift else tiles[j]
            merged = turned if merged is None else jnp.where(group == j, turned, merged)
        results.append(merged)
    return results


def route(tiles_ref, count_ref, rows_ref, *rest):
    out_ref, held = rest[-2:]
    own = lax.axis_index("owner")
    list_len = tiles_ref.shape[1]
    held[...] = jnp.zeros_like(held)
    count = count_ref[own]
    for place in range(list_len):
        owner = tiles_ref[own, place] // 2
        held[owner] += jnp.where(place < count, rows_ref[place].astype(jnp.float32), 0.0)
    width = LANE // NX
    group = lane_group((SUB, LANE), width)
    for z in range(NZ):
        for core in range(NC):
            tiles = [held[owner_index(z, x, core)] for x in range(NX)]
            for x in range(NX):
                wanted = [(tiles[x ^ (3 * a)], x ^ d) for a in range(2) for d in range(2)]
                merged = None
                for place, (tile, spot) in enumerate(wanted):
                    shift = (place - spot) % NX * width
                    turned = pltpu.roll(tile, shift, 1) if shift else tile
                    merged = turned if merged is None else jnp.where(group == place, turned, merged)
                out_ref[owner_index(z, x, core)] = merged.astype(out_ref.dtype)


def accumulate(ab_ref, ab_count_ref, cd_ref, cd_count_ref, rows_ref, *rest):
    out_ref, mask = rest[-2:]
    own, piece = lax.axis_index("owner"), lax.axis_index("blk")
    chunk = piece % (NZ * NC)
    z, x, core = own // (NX * NC), (own // NC) % NX, own % NC
    tasks, list_len = ab_ref.shape
    place = lax.broadcasted_iota(jnp.int32, (tasks, list_len), 1)
    task = lax.broadcasted_iota(jnp.int32, (tasks, tasks), 0)
    same = task == lax.broadcasted_iota(jnp.int32, (tasks, tasks), 1)

    def live(list_ref, count_ref):
        counts = jnp.where(same, count_ref[...].astype(jnp.float32), 0.0)
        counts = jnp.sum(counts, axis=1, keepdims=True)
        return jnp.where(place.astype(jnp.float32) < counts, list_ref[...], -1)

    ab_list, cd_list = live(ab_ref, ab_count_ref), live(cd_ref, cd_count_ref)
    group = lane_group((tasks, LANE), LANE // NX)

    def hit(tile_list, tile):
        return jnp.max((tile_list == tile).astype(jnp.float32), axis=1, keepdims=True)

    def ab_hit(low):
        mine, theirs = (hit(ab_list, owner_index(z, spot, core) * 2 + low) for spot in (x, x ^ 3))
        return jnp.where(group < 2, mine, theirs)

    def cd_hit(par):
        mine, theirs = (
            hit(cd_list, owner_index(chunk // NC, spot, chunk % NC) * 2 + par) for spot in (x, x ^ 1)
        )
        return jnp.where(group % 2 == 0, mine, theirs)

    cd_hits = [cd_hit(par) for par in range(2)]
    for low in range(2):
        rows_hit = ab_hit(low)
        for par in range(2):
            mask[low * 2 + par] = rows_hit * cd_hits[par]
    totals = [jnp.zeros((SUB, LANE), jnp.float32) for _ in range(4)]
    for task in range(tasks):
        rows = rows_ref[task].astype(jnp.float32)
        for kind in range(4):
            totals[kind] += rows * mask[kind, task : task + 1, :]
    for kind in range(4):
        rounded = totals[kind].astype(out_ref.dtype)
        for target in range(out_ref.shape[0]):
            out_ref[target, kind] = rounded


def collect_near(own_ref, first_ref, second_ref, near_ref, relay_ref):
    for place, ref in enumerate((own_ref, first_ref, second_ref)):
        near_ref[place] = ref[...]
    relay_ref[...] = first_ref[...]


def settle(*refs):
    pass


def collect_all(near_ref, far_ref, out_ref):
    out_ref[: NZ - 1] = near_ref[...]
    out_ref[NZ - 1] = far_ref[...]


def multiply(weights_ref, *rest):
    amps_refs, (mine_ref, theirs_ref, left) = rest[:4], rest[4:]
    own = lax.axis_index("owner")
    z, core = own // (NX * NC), own % NC
    width, occ = amps_refs[0].shape[2:]
    chunks = NZ * NC
    blocks = [(par, d, side) for par in range(2) for d in range(2) for side in range(NC)]
    for kind in range(4):
        low, par = kind // 2, kind % 2
        for side in range(NC):
            parts = []
            for part in range(width // SUB):
                tiles = []
                for step in STEPS:
                    chunk = (z ^ step) * NC + (core + side) % NC
                    tiles.append(weights_ref[part * chunks + chunk, kind].astype(jnp.float32))
                parts.append(regroup(tiles, width))
            for a in range(2):
                for d in range(2):
                    rows = jnp.concatenate([p[2 * a + d] for p in parts], axis=0)
                    row, col = (a * 2 + low) * width, blocks.index((par, d, side)) * LANE
                    left[row : row + width, col : col + LANE] = rows.astype(left.dtype)
    wide = 256
    for col in range(0, occ, wide):
        total = None
        for at, (par, d, side) in enumerate(blocks):
            right = amps_refs[2 * side + d][:, par, :, col : col + wide].reshape(LANE, wide)
            term = jnp.dot(left[:, at * LANE : (at + 1) * LANE], right, preferred_element_type=jnp.float32)
            total = term if total is None else total + term
        mine_ref[:, col : col + wide] = total[: 2 * width]
        theirs_ref[:, col : col + wide] = total[2 * width :]


def moved(block, dz=0, dx=0, dcore=0):
    pairs = [
        (owner_index(z, x, core), owner_index(z ^ dz, x ^ dx, core ^ dcore))
        for z in range(NZ)
        for x in range(NX)
        for core in range(NC)
    ]
    return lax.ppermute(block, "owner", pairs)


def joined(near, far, flops):
    return pl.pallas_call(
        collect_all,
        out_shape=jax.ShapeDtypeStruct((near.shape[0] + 1, *near.shape[1:]), near.dtype),
        in_specs=[VMEM] * 2,
        out_specs=VMEM,
        cost_estimate=pl.CostEstimate(flops=flops, bytes_accessed=near.size * 6, transcendentals=0),
        compiler_params=SMALL,
        name="collect_all",
    )(near, far)


def shards(amplitudes, integrals, cd_tiles, cd_count, ab_tiles, ab_count):
    tile_dev, width, occ = amplitudes.shape
    owners, pieces = lax.axis_size("owner"), lax.axis_size("blk")
    tasks = cd_tiles.shape[0]
    bf16, f32 = jnp.bfloat16, jnp.float32

    first, second = moved(amplitudes, 1), moved(amplitudes, 3)
    ordered = pl.pallas_call(
        order_columns,
        out_shape=jax.ShapeDtypeStruct((width // SUB, NZ * NC, SUB, LANE), bf16),
        in_specs=[SMEM, SMEM, VMEM],
        out_specs=VMEM,
        scratch_shapes=[pltpu.VMEM((NZ * NC, width, LANE), f32)],
        name="order_columns",
    )(cd_tiles, cd_count, integrals[0])
    ordered = ordered.reshape(pieces, SUB, LANE)
    mine = lax.all_to_all(ordered, "blk", split_axis=0, concat_axis=0, tiled=True)
    outgoing = pl.pallas_call(
        route,
        out_shape=jax.ShapeDtypeStruct((owners, SUB, LANE), bf16),
        in_specs=[SMEM, SMEM, VMEM],
        out_specs=VMEM,
        scratch_shapes=[pltpu.VMEM((owners, SUB, LANE), f32)],
        compiler_params=SMALL,
        name="route",
    )(ab_tiles, ab_count, mine)
    near, relay = pl.pallas_call(
        collect_near,
        out_shape=(
            jax.ShapeDtypeStruct((NZ - 1, tile_dev, width, occ), bf16),
            jax.ShapeDtypeStruct(second.shape, bf16),
        ),
        in_specs=[VMEM] * 3,
        out_specs=(VMEM, VMEM),
        cost_estimate=pl.CostEstimate(flops=10000000000, bytes_accessed=amplitudes.size * 16, transcendentals=0),
        compiler_params=SMALL,
        name="collect_near",
    )(amplitudes, first, second)
    near_pair = moved(near, dx=1)
    far = moved(relay, 3)
    arrived = lax.all_to_all(outgoing, "owner", split_axis=0, concat_axis=0, tiled=True)
    spread = pl.pallas_call(
        accumulate,
        out_shape=jax.ShapeDtypeStruct((pieces, 4, SUB, LANE), bf16),
        in_specs=[VMEM] * 5,
        out_specs=VMEM,
        scratch_shapes=[pltpu.VMEM((4, tasks, LANE), f32)],
        compiler_params=SMALL,
        name="accumulate",
    )(ab_tiles, ab_count[None, :], cd_tiles, cd_count[None, :], arrived)
    far = pl.pallas_call(
        settle,
        out_shape=jax.ShapeDtypeStruct(far.shape, far.dtype),
        in_specs=[ANY, ANY],
        out_specs=ANY,
        input_output_aliases={0: 0},
        cost_estimate=pl.CostEstimate(flops=1000000, bytes_accessed=far.size * 4, transcendentals=0),
        compiler_params=SMALL,
        name="settle",
    )(far, spread)
    far_pair = moved(far, dx=1)
    sides = [joined(near, far, 2000000000), joined(near_pair, far_pair, 5000000000)]
    sides += [moved(side, dcore=1) for side in sides]

    weights = lax.all_to_all(spread, "blk", split_axis=0, concat_axis=0, tiled=True)
    half = jax.ShapeDtypeStruct((tile_dev * width, occ), f32)
    mine, theirs = pl.pallas_call(
        multiply,
        out_shape=(half, half),
        in_specs=[VMEM] * 5,
        out_specs=(VMEM, VMEM),
        scratch_shapes=[pltpu.VMEM((2 * tile_dev * width, 2 * NZ * NC * tile_dev * width), bf16)],
        compiler_params=pltpu.CompilerParams(vmem_limit_bytes=16 * 1024 * 1024),
        name="multiply",
    )(weights, *sides)
    return (mine + moved(theirs, dx=3)).reshape(tile_dev, width, occ)


def solution(mesh):
    placed = (P("owner", None, "blk"), P("owner", "blk", None), P(), P(), P(), P())
    return jax.shard_map(
        shards, mesh=mesh, in_specs=placed, out_specs=P("owner", None, "blk"), check_vma=False
    )
```

```python
import functools

import jax
import jax.numpy as jnp
from jax import lax
from jax.experimental import pallas as pl
from jax.experimental.pallas import tpu as pltpu
from jax.sharding import PartitionSpec as P

NZ, NX, NC = 4, 4, 2
SUB, LANE = 8, 128
SMEM = pl.BlockSpec(memory_space=pltpu.SMEM)
VMEM = pl.BlockSpec(memory_space=pltpu.VMEM)
ANY = pl.BlockSpec(memory_space=pl.ANY)
SMALL = pltpu.CompilerParams(vmem_limit_bytes=4 * 1024 * 1024)
STEPS = (0, 1, 3, 2)


def owner_index(z, x, core):
    return (z * NX + x) * NC + core


def lane_group(shape, width):
    return lax.broadcasted_iota(jnp.int32, shape, len(shape) - 1) // width


def order_columns(tiles_ref, count_ref, rows_ref, out_ref, total):
    own = lax.axis_index("owner")
    width, columns = rows_ref.shape
    list_len = tiles_ref.shape[1]
    groups = LANE // width
    total[...] = jnp.zeros_like(total)
    count = count_ref[own]
    group = lane_group((width, LANE), width)
    for place in range(list_len):
        if place % groups == 0:
            chunk = rows_ref[:, place // groups * LANE : (place // groups + 1) * LANE].astype(jnp.float32)
        owner = tiles_ref[own, place] // 2
        spot = (owner // NC) % NX
        target = owner // (NX * NC) * NC + owner % NC
        turned = pltpu.roll(chunk, (spot - place % groups + groups) % groups * width, 1)
        keep = (group == spot) & (place < count)
        total[target] += jnp.where(keep, turned, 0.0)
    for part in range(width // SUB):
        for target in range(NZ * NC):
            out_ref[part, target] = total[target, part * SUB : (part + 1) * SUB, :].astype(out_ref.dtype)


def regroup(tiles, width):
    count = len(tiles)
    group = lane_group(tiles[0].shape, width)
    results = []
    for i in range(count):
        merged = None
        for j in range(count):
            shift = (j - i) % count * width
            turned = pltpu.roll(tiles[j], shift, tiles[j].ndim - 1) if shift else tiles[j]
            merged = turned if merged is None else jnp.where(group == j, turned, merged)
        results.append(merged)
    return results


def route(tiles_ref, count_ref, rows_ref, *rest):
    out_ref, held = rest[-2:]
    own = lax.axis_index("owner")
    list_len = tiles_ref.shape[1]
    held[...] = jnp.zeros_like(held)
    count = count_ref[own]
    for place in range(list_len):
        owner = tiles_ref[own, place] // 2
        held[owner] += jnp.where(place < count, rows_ref[place].astype(jnp.float32), 0.0)
    width = LANE // NX
    group = lane_group((SUB, LANE), width)
    for z in range(NZ):
        for core in range(NC):
            tiles = [held[owner_index(z, x, core)] for x in range(NX)]
            for x in range(NX):
                wanted = [(tiles[x ^ (3 * a)], x ^ d) for a in range(2) for d in range(2)]
                merged = None
                for place, (tile, spot) in enumerate(wanted):
                    shift = (place - spot) % NX * width
                    turned = pltpu.roll(tile, shift, 1) if shift else tile
                    merged = turned if merged is None else jnp.where(group == place, turned, merged)
                out_ref[owner_index(z, x, core)] = merged.astype(out_ref.dtype)


def accumulate(ab_ref, ab_count_ref, cd_ref, cd_count_ref, rows_ref, *rest):
    out_ref, mask = rest[-2:]
    own, piece = lax.axis_index("owner"), lax.axis_index("blk")
    chunk = piece % (NZ * NC)
    z, x, core = own // (NX * NC), (own // NC) % NX, own % NC
    tasks, list_len = ab_ref.shape
    place = lax.broadcasted_iota(jnp.int32, (tasks, list_len), 1)
    task = lax.broadcasted_iota(jnp.int32, (tasks, tasks), 0)
    same = task == lax.broadcasted_iota(jnp.int32, (tasks, tasks), 1)

    def live(list_ref, count_ref):
        counts = jnp.where(same, count_ref[...].astype(jnp.float32), 0.0)
        counts = jnp.sum(counts, axis=1, keepdims=True)
        return jnp.where(place.astype(jnp.float32) < counts, list_ref[...], -1)

    ab_list, cd_list = live(ab_ref, ab_count_ref), live(cd_ref, cd_count_ref)
    group = lane_group((tasks, LANE), LANE // NX)

    def hit(tile_list, tile):
        return jnp.max((tile_list == tile).astype(jnp.float32), axis=1, keepdims=True)

    def ab_hit(low):
        mine, theirs = (hit(ab_list, owner_index(z, spot, core) * 2 + low) for spot in (x, x ^ 3))
        return jnp.where(group < 2, mine, theirs)

    def cd_hit(par):
        mine, theirs = (
            hit(cd_list, owner_index(chunk // NC, spot, chunk % NC) * 2 + par) for spot in (x, x ^ 1)
        )
        return jnp.where(group % 2 == 0, mine, theirs)

    cd_hits = [cd_hit(par) for par in range(2)]
    for low in range(2):
        rows_hit = ab_hit(low)
        for par in range(2):
            mask[low * 2 + par] = rows_hit * cd_hits[par]
    totals = [jnp.zeros((SUB, LANE), jnp.float32) for _ in range(4)]
    for task in range(tasks):
        rows = rows_ref[task].astype(jnp.float32)
        for kind in range(4):
            totals[kind] += rows * mask[kind, task : task + 1, :]
    for kind in range(4):
        rounded = totals[kind].astype(out_ref.dtype)
        for target in range(out_ref.shape[0]):
            out_ref[target, kind] = rounded


def collect_near(own_ref, first_ref, second_ref, near_ref, relay_ref):
    for place, ref in enumerate((own_ref, first_ref, second_ref)):
        near_ref[place] = ref[...]
    relay_ref[...] = first_ref[...]


def settle(*refs):
    pass


def collect_all(near_ref, far_ref, out_ref):
    out_ref[: NZ - 1] = near_ref[...]
    out_ref[NZ - 1] = far_ref[...]


def multiply(weights_ref, *rest):
    amps_refs, (mine_ref, theirs_ref, left) = rest[:4], rest[4:]
    own = lax.axis_index("owner")
    z, core = own // (NX * NC), own % NC
    width, occ = amps_refs[0].shape[2:]
    chunks = NZ * NC
    blocks = [(par, d, side) for par in range(2) for d in range(2) for side in range(NC)]
    for kind in range(4):
        low, par = kind // 2, kind % 2
        for side in range(NC):
            parts = []
            for part in range(width // SUB):
                tiles = []
                for step in STEPS:
                    chunk = (z ^ step) * NC + (core + side) % NC
                    tiles.append(weights_ref[part * chunks + chunk, kind].astype(jnp.float32))
                parts.append(regroup(tiles, width))
            for a in range(2):
                for d in range(2):
                    rows = jnp.concatenate([p[2 * a + d] for p in parts], axis=0)
                    row, col = (a * 2 + low) * width, blocks.index((par, d, side)) * LANE
                    left[row : row + width, col : col + LANE] = rows.astype(left.dtype)
    wide = 256
    for col in range(0, occ, wide):
        total = None
        for at, (par, d, side) in enumerate(blocks):
            right = amps_refs[2 * side + d][:, par, :, col : col + wide].reshape(LANE, wide)
            term = jnp.dot(left[:, at * LANE : (at + 1) * LANE], right, preferred_element_type=jnp.float32)
            total = term if total is None else total + term
        mine_ref[:, col : col + wide] = total[: 2 * width]
        theirs_ref[:, col : col + wide] = total[2 * width :].astype(theirs_ref.dtype)


def moved(block, dz=0, dx=0, dcore=0):
    pairs = [
        (owner_index(z, x, core), owner_index(z ^ dz, x ^ dx, core ^ dcore))
        for z in range(NZ)
        for x in range(NX)
        for core in range(NC)
    ]
    return lax.ppermute(block, "owner", pairs)


def joined(near, far, flops):
    return pl.pallas_call(
        collect_all,
        out_shape=jax.ShapeDtypeStruct((near.shape[0] + 1, *near.shape[1:]), near.dtype),
        in_specs=[VMEM] * 2,
        out_specs=VMEM,
        cost_estimate=pl.CostEstimate(flops=flops, bytes_accessed=near.size * 6, transcendentals=0),
        compiler_params=SMALL,
        name="collect_all",
    )(near, far)


def shards(amplitudes, integrals, cd_tiles, cd_count, ab_tiles, ab_count):
    tile_dev, width, occ = amplitudes.shape
    owners, pieces = lax.axis_size("owner"), lax.axis_size("blk")
    tasks = cd_tiles.shape[0]
    bf16, f32 = jnp.bfloat16, jnp.float32

    first, second = moved(amplitudes, 1), moved(amplitudes, 3)
    ordered = pl.pallas_call(
        order_columns,
        out_shape=jax.ShapeDtypeStruct((width // SUB, NZ * NC, SUB, LANE), bf16),
        in_specs=[SMEM, SMEM, VMEM],
        out_specs=VMEM,
        scratch_shapes=[pltpu.VMEM((NZ * NC, width, LANE), f32)],
        name="order_columns",
    )(cd_tiles, cd_count, integrals[0])
    ordered = ordered.reshape(pieces, SUB, LANE)
    mine = lax.all_to_all(ordered, "blk", split_axis=0, concat_axis=0, tiled=True)
    outgoing = pl.pallas_call(
        route,
        out_shape=jax.ShapeDtypeStruct((owners, SUB, LANE), bf16),
        in_specs=[SMEM, SMEM, VMEM],
        out_specs=VMEM,
        scratch_shapes=[pltpu.VMEM((owners, SUB, LANE), f32)],
        compiler_params=SMALL,
        name="route",
    )(ab_tiles, ab_count, mine)
    near, relay = pl.pallas_call(
        collect_near,
        out_shape=(
            jax.ShapeDtypeStruct((NZ - 1, tile_dev, width, occ), bf16),
            jax.ShapeDtypeStruct(second.shape, bf16),
        ),
        in_specs=[VMEM] * 3,
        out_specs=(VMEM, VMEM),
        cost_estimate=pl.CostEstimate(flops=10000000000, bytes_accessed=amplitudes.size * 16, transcendentals=0),
        compiler_params=SMALL,
        name="collect_near",
    )(amplitudes, first, second)
    near_pair = moved(near, dx=1)
    far = moved(relay, 3)
    arrived = lax.all_to_all(outgoing, "owner", split_axis=0, concat_axis=0, tiled=True)
    spread = pl.pallas_call(
        accumulate,
        out_shape=jax.ShapeDtypeStruct((pieces, 4, SUB, LANE), bf16),
        in_specs=[VMEM] * 5,
        out_specs=VMEM,
        scratch_shapes=[pltpu.VMEM((4, tasks, LANE), f32)],
        compiler_params=SMALL,
        name="accumulate",
    )(ab_tiles, ab_count[None, :], cd_tiles, cd_count[None, :], arrived)
    far = pl.pallas_call(
        settle,
        out_shape=jax.ShapeDtypeStruct(far.shape, far.dtype),
        in_specs=[ANY, ANY],
        out_specs=ANY,
        input_output_aliases={0: 0},
        cost_estimate=pl.CostEstimate(flops=1000000, bytes_accessed=far.size * 4, transcendentals=0),
        compiler_params=SMALL,
        name="settle",
    )(far, spread)
    far_pair = moved(far, dx=1)
    sides = [joined(near, far, 2000000000), joined(near_pair, far_pair, 5000000000)]
    sides += [moved(side, dcore=1) for side in sides]

    weights = lax.all_to_all(spread, "blk", split_axis=0, concat_axis=0, tiled=True)
    shape = (tile_dev * width, occ)
    mine, theirs = pl.pallas_call(
        multiply,
        out_shape=(jax.ShapeDtypeStruct(shape, f32), jax.ShapeDtypeStruct(shape, bf16)),
        in_specs=[VMEM] * 5,
        out_specs=(VMEM, VMEM),
        scratch_shapes=[pltpu.VMEM((2 * tile_dev * width, 2 * NZ * NC * tile_dev * width), bf16)],
        compiler_params=pltpu.CompilerParams(vmem_limit_bytes=16 * 1024 * 1024),
        name="multiply",
    )(weights, *sides)
    return (mine + moved(theirs, dx=3).astype(f32)).reshape(tile_dev, width, occ)


def solution(mesh):
    placed = (P("owner", None, "blk"), P("owner", "blk", None), P(), P(), P(), P())
    return jax.shard_map(
        shards, mesh=mesh, in_specs=placed, out_specs=P("owner", None, "blk"), check_vma=False
    )
```

```python
import functools

import jax
import jax.numpy as jnp
from jax import lax
from jax.experimental import pallas as pl
from jax.experimental.pallas import tpu as pltpu
from jax.sharding import PartitionSpec as P

NZ, NX, NC = 4, 4, 2
SUB, LANE = 8, 128
SMEM = pl.BlockSpec(memory_space=pltpu.SMEM)
VMEM = pl.BlockSpec(memory_space=pltpu.VMEM)
ANY = pl.BlockSpec(memory_space=pl.ANY)
SMALL = pltpu.CompilerParams(vmem_limit_bytes=4 * 1024 * 1024)
STEPS = (0, 1, 3, 2)


def owner_index(z, x, core):
    return (z * NX + x) * NC + core


def lane_group(shape, width):
    return lax.broadcasted_iota(jnp.int32, shape, len(shape) - 1) // width


def order_columns(tiles_ref, count_ref, rows_ref, out_ref, total):
    own = lax.axis_index("owner")
    width, columns = rows_ref.shape
    list_len = tiles_ref.shape[1]
    groups = LANE // width
    total[...] = jnp.zeros_like(total)
    count = count_ref[own]
    group = lane_group((width, LANE), width)
    for place in range(list_len):
        if place % groups == 0:
            chunk = rows_ref[:, place // groups * LANE : (place // groups + 1) * LANE].astype(jnp.float32)
        owner = tiles_ref[own, place] // 2
        spot = (owner // NC) % NX
        target = owner // (NX * NC) * NC + owner % NC
        turned = pltpu.roll(chunk, (spot - place % groups + groups) % groups * width, 1)
        keep = (group == spot) & (place < count)
        total[target] += jnp.where(keep, turned, 0.0)
    for part in range(width // SUB):
        for target in range(NZ * NC):
            out_ref[part, target] = total[target, part * SUB : (part + 1) * SUB, :].astype(out_ref.dtype)


def regroup(tiles, width):
    count = len(tiles)
    group = lane_group(tiles[0].shape, width)
    results = []
    for i in range(count):
        merged = None
        for j in range(count):
            shift = (j - i) % count * width
            turned = pltpu.roll(tiles[j], shift, tiles[j].ndim - 1) if shift else tiles[j]
            merged = turned if merged is None else jnp.where(group == j, turned, merged)
        results.append(merged)
    return results


def route(tiles_ref, count_ref, rows_ref, *rest):
    out_ref, held = rest[-2:]
    own = lax.axis_index("owner")
    list_len = tiles_ref.shape[1]
    held[...] = jnp.zeros_like(held)
    count = count_ref[own]
    for place in range(list_len):
        owner = tiles_ref[own, place] // 2
        held[owner] += jnp.where(place < count, rows_ref[place].astype(jnp.float32), 0.0)
    width = LANE // NX
    group = lane_group((SUB, LANE), width)
    for z in range(NZ):
        for core in range(NC):
            tiles = [held[owner_index(z, x, core)] for x in range(NX)]
            for x in range(NX):
                wanted = [(tiles[x ^ (3 * a)], x ^ d) for a in range(2) for d in range(2)]
                merged = None
                for place, (tile, spot) in enumerate(wanted):
                    shift = (place - spot) % NX * width
                    turned = pltpu.roll(tile, shift, 1) if shift else tile
                    merged = turned if merged is None else jnp.where(group == place, turned, merged)
                out_ref[owner_index(z, x, core)] = merged.astype(out_ref.dtype)


def make_masks(ab_ref, ab_count_ref, cd_ref, cd_count_ref, mask):
    own, piece = lax.axis_index("owner"), lax.axis_index("blk")
    chunk = piece % (NZ * NC)
    z, x, core = own // (NX * NC), (own // NC) % NX, own % NC
    tasks, list_len = ab_ref.shape
    place = lax.broadcasted_iota(jnp.int32, (tasks, list_len), 1)
    task = lax.broadcasted_iota(jnp.int32, (tasks, tasks), 0)
    same = task == lax.broadcasted_iota(jnp.int32, (tasks, tasks), 1)

    def live(list_ref, count_ref):
        counts = jnp.where(same, count_ref[...].astype(jnp.float32), 0.0)
        counts = jnp.sum(counts, axis=1, keepdims=True)
        return jnp.where(place.astype(jnp.float32) < counts, list_ref[...], -1)

    ab_list, cd_list = live(ab_ref, ab_count_ref), live(cd_ref, cd_count_ref)
    group = lane_group((tasks, LANE), LANE // NX)

    def hit(tile_list, tile):
        return jnp.max((tile_list == tile).astype(jnp.float32), axis=1, keepdims=True)

    def ab_hit(low):
        mine, theirs = (hit(ab_list, owner_index(z, spot, core) * 2 + low) for spot in (x, x ^ 3))
        return jnp.where(group < 2, mine, theirs)

    def cd_hit(par):
        mine, theirs = (
            hit(cd_list, owner_index(chunk // NC, spot, chunk % NC) * 2 + par) for spot in (x, x ^ 1)
        )
        return jnp.where(group % 2 == 0, mine, theirs)

    cd_hits = [cd_hit(par) for par in range(2)]
    for low in range(2):
        rows_hit = ab_hit(low)
        for par in range(2):
            mask[low * 2 + par] = rows_hit * cd_hits[par]


def accumulate(mask, rows_ref, out_ref):
    totals = [jnp.zeros((SUB, LANE), jnp.float32) for _ in range(4)]
    for task in range(rows_ref.shape[0]):
        rows = rows_ref[task].astype(jnp.float32)
        for kind in range(4):
            totals[kind] += rows * mask[kind, task : task + 1, :]
    for kind in range(4):
        rounded = totals[kind].astype(out_ref.dtype)
        for target in range(out_ref.shape[0]):
            out_ref[target, kind] = rounded


def collect_near(*refs):
    own_ref, first_ref, second_ref, _ = refs[:4]
    near_ref, relay_ref, mask = refs[8:]
    make_masks(*refs[4:8], mask)
    for place, ref in enumerate((own_ref, first_ref, second_ref)):
        near_ref[place] = ref[...]
    relay_ref[...] = first_ref[...]


def settle(*refs):
    pass


def collect_rest(near_pair_ref, far_ref, far_pair_ref, _, out_ref):
    out_ref[: NZ - 1] = near_pair_ref[...]
    out_ref[NZ - 1] = far_ref[...]
    out_ref[NZ] = far_pair_ref[...]


def multiply(weights_ref, *rest):
    mine_ref, theirs_ref, left = rest[4:]
    amps = [((near, more, NZ - 1), (more, more, NZ)) for near, more in (rest[:2], rest[2:4])]
    own = lax.axis_index("owner")
    z, core = own // (NX * NC), own % NC
    width, occ = rest[0].shape[2:]
    chunks = NZ * NC
    blocks = [(par, d, side) for par in range(2) for d in range(2) for side in range(NC)]
    for kind in range(4):
        low, par = kind // 2, kind % 2
        for side in range(NC):
            parts = []
            for part in range(width // SUB):
                tiles = []
                for step in STEPS:
                    chunk = (z ^ step) * NC + (core + side) % NC
                    tiles.append(weights_ref[part * chunks + chunk, kind].astype(jnp.float32))
                parts.append(regroup(tiles, width))
            for a in range(2):
                for d in range(2):
                    rows = jnp.concatenate([p[2 * a + d] for p in parts], axis=0)
                    row, col = (a * 2 + low) * width, blocks.index((par, d, side)) * LANE
                    left[row : row + width, col : col + LANE] = rows.astype(left.dtype)
    wide = 256
    for col in range(0, occ, wide):
        total = None
        for at, (par, d, side) in enumerate(blocks):
            near, far, last = amps[side][d]
            right = [ref[place, par, :, col : col + wide] for ref, place in ((near, 0), (near, 1), (near, 2), (far, last))]
            right = jnp.concatenate(right, axis=0)
            term = jnp.dot(left[:, at * LANE : (at + 1) * LANE], right, preferred_element_type=jnp.float32)
            total = term if total is None else total + term
        mine_ref[:, col : col + wide] = total[: 2 * width]
        theirs_ref[:, col : col + wide] = total[2 * width :].astype(theirs_ref.dtype)


def moved(block, dz=0, dx=0, dcore=0):
    pairs = [
        (owner_index(z, x, core), owner_index(z ^ dz, x ^ dx, core ^ dcore))
        for z in range(NZ)
        for x in range(NX)
        for core in range(NC)
    ]
    return lax.ppermute(block, "owner", pairs)


def shards(amplitudes, integrals, cd_tiles, cd_count, ab_tiles, ab_count):
    tile_dev, width, occ = amplitudes.shape
    owners, pieces = lax.axis_size("owner"), lax.axis_size("blk")
    tasks = cd_tiles.shape[0]
    bf16, f32 = jnp.bfloat16, jnp.float32

    first, second = moved(amplitudes, 1), moved(amplitudes, 3)
    ordered = pl.pallas_call(
        order_columns,
        out_shape=jax.ShapeDtypeStruct((width // SUB, NZ * NC, SUB, LANE), bf16),
        in_specs=[SMEM, SMEM, VMEM],
        out_specs=VMEM,
        scratch_shapes=[pltpu.VMEM((NZ * NC, width, LANE), f32)],
        name="order_columns",
    )(cd_tiles, cd_count, integrals[0])
    ordered = ordered.reshape(pieces, SUB, LANE)
    mine = lax.all_to_all(ordered, "blk", split_axis=0, concat_axis=0, tiled=True)
    outgoing = pl.pallas_call(
        route,
        out_shape=jax.ShapeDtypeStruct((owners, SUB, LANE), bf16),
        in_specs=[SMEM, SMEM, VMEM],
        out_specs=VMEM,
        scratch_shapes=[pltpu.VMEM((owners, SUB, LANE), f32)],
        compiler_params=SMALL,
        name="route",
    )(ab_tiles, ab_count, mine)
    near, relay, mask = pl.pallas_call(
        collect_near,
        out_shape=(
            jax.ShapeDtypeStruct((NZ - 1, tile_dev, width, occ), bf16),
            jax.ShapeDtypeStruct(second.shape, bf16),
            jax.ShapeDtypeStruct((4, tasks, LANE), f32),
        ),
        in_specs=[VMEM] * 3 + [ANY] + [VMEM] * 4,
        out_specs=(VMEM, VMEM, VMEM),
        cost_estimate=pl.CostEstimate(flops=10000000000, bytes_accessed=amplitudes.size * 16, transcendentals=0),
        compiler_params=SMALL,
        name="collect_near",
    )(amplitudes, first, second, mine, ab_tiles, ab_count[None, :], cd_tiles, cd_count[None, :])
    near_pair = moved(near, dx=1)
    near_other = moved(near, dcore=1)
    far = moved(relay, 3)
    arrived = lax.all_to_all(outgoing, "owner", split_axis=0, concat_axis=0, tiled=True)
    spread = pl.pallas_call(
        accumulate,
        out_shape=jax.ShapeDtypeStruct((pieces, 4, SUB, LANE), bf16),
        in_specs=[VMEM] * 2,
        out_specs=VMEM,
        compiler_params=SMALL,
        name="accumulate",
    )(mask, arrived)
    far = pl.pallas_call(
        settle,
        out_shape=jax.ShapeDtypeStruct(far.shape, far.dtype),
        in_specs=[ANY, ANY],
        out_specs=ANY,
        input_output_aliases={0: 0},
        cost_estimate=pl.CostEstimate(flops=2000000000, bytes_accessed=far.size * 4, transcendentals=0),
        compiler_params=SMALL,
        name="settle",
    )(far, spread)
    far_pair = moved(far, dx=1)
    rest = pl.pallas_call(
        collect_rest,
        out_shape=jax.ShapeDtypeStruct((NZ + 1, tile_dev, width, occ), bf16),
        in_specs=[VMEM] * 3 + [ANY],
        out_specs=VMEM,
        cost_estimate=pl.CostEstimate(flops=2000000000, bytes_accessed=amplitudes.size * 20, transcendentals=0),
        compiler_params=SMALL,
        name="collect_rest",
    )(near_pair, far, far_pair, near_other)
    sides = [near, rest, near_other, moved(rest, dcore=1)]

    weights = lax.all_to_all(spread, "blk", split_axis=0, concat_axis=0, tiled=True)
    shape = (tile_dev * width, occ)
    mine, theirs = pl.pallas_call(
        multiply,
        out_shape=(jax.ShapeDtypeStruct(shape, f32), jax.ShapeDtypeStruct(shape, bf16)),
        in_specs=[VMEM] * 5,
        out_specs=(VMEM, VMEM),
        scratch_shapes=[pltpu.VMEM((2 * tile_dev * width, 2 * NZ * NC * tile_dev * width), bf16)],
        compiler_params=pltpu.CompilerParams(vmem_limit_bytes=16 * 1024 * 1024),
        name="multiply",
    )(weights, *sides)
    return (mine + moved(theirs, dx=3).astype(f32)).reshape(tile_dev, width, occ)


def solution(mesh):
    placed = (P("owner", None, "blk"), P("owner", "blk", None), P(), P(), P(), P())
    return jax.shard_map(
        shards, mesh=mesh, in_specs=placed, out_specs=P("owner", None, "blk"), check_vma=False
    )
```

```python
import functools

import jax
import jax.numpy as jnp
from jax import lax
from jax.experimental import pallas as pl
from jax.experimental.pallas import tpu as pltpu
from jax.sharding import PartitionSpec as P

NZ, NX, NC = 4, 4, 2
SUB, LANE = 8, 128
SMEM = pl.BlockSpec(memory_space=pltpu.SMEM)
VMEM = pl.BlockSpec(memory_space=pltpu.VMEM)
ANY = pl.BlockSpec(memory_space=pl.ANY)
SMALL = pltpu.CompilerParams(vmem_limit_bytes=4 * 1024 * 1024)
STEPS = (0, 1, 3, 2)


def owner_index(z, x, core):
    return (z * NX + x) * NC + core


def lane_group(shape, width):
    return lax.broadcasted_iota(jnp.int32, shape, len(shape) - 1) // width


def invert(tiles_ref, count_ref, where_ref):
    own = lax.axis_index("owner")
    for owner in range(where_ref.shape[0]):
        where_ref[owner] = -1
    count = count_ref[own]
    for place in range(tiles_ref.shape[1]):
        owner = tiles_ref[own, place] // 2

        @pl.when(place < count)
        def _():
            where_ref[owner] = place


def order_columns(tiles_ref, count_ref, rows_ref, out_ref, where_ref):
    width = rows_ref.shape[0]
    groups = LANE // width
    invert(tiles_ref, count_ref, where_ref)
    group = lane_group((width, LANE), width)
    for z in range(NZ):
        for core in range(NC):
            merged = jnp.zeros((width, LANE), jnp.float32)
            for spot in range(NX):
                found = where_ref[owner_index(z, spot, core)]
                place = jnp.maximum(found, 0)
                start = pl.multiple_of(place // groups * LANE, LANE)
                chunk = rows_ref[:, pl.ds(start, LANE)].astype(jnp.float32)
                turned = pltpu.roll(chunk, (spot - place % groups + groups) % groups * width, 1)
                merged = jnp.where((group == spot) & (found >= 0), turned, merged)
            for part in range(width // SUB):
                out_ref[part, z * NC + core] = merged[part * SUB : (part + 1) * SUB].astype(out_ref.dtype)


def regroup(tiles, width):
    count = len(tiles)
    group = lane_group(tiles[0].shape, width)
    results = []
    for i in range(count):
        merged = None
        for j in range(count):
            shift = (j - i) % count * width
            turned = pltpu.roll(tiles[j], shift, tiles[j].ndim - 1) if shift else tiles[j]
            merged = turned if merged is None else jnp.where(group == j, turned, merged)
        results.append(merged)
    return results


def route(tiles_ref, count_ref, rows_ref, out_ref, where_ref):
    invert(tiles_ref, count_ref, where_ref)

    def held(owner):
        found = where_ref[owner]
        return jnp.where(found >= 0, rows_ref[jnp.maximum(found, 0)].astype(jnp.float32), 0.0)

    width = LANE // NX
    group = lane_group((SUB, LANE), width)
    for z in range(NZ):
        for core in range(NC):
            tiles = [held(owner_index(z, x, core)) for x in range(NX)]
            for x in range(NX):
                wanted = [(tiles[x ^ (3 * a)], x ^ d) for a in range(2) for d in range(2)]
                merged = None
                for place, (tile, spot) in enumerate(wanted):
                    shift = (place - spot) % NX * width
                    turned = pltpu.roll(tile, shift, 1) if shift else tile
                    merged = turned if merged is None else jnp.where(group == place, turned, merged)
                out_ref[owner_index(z, x, core)] = merged.astype(out_ref.dtype)


def make_masks(ab_ref, ab_count_ref, cd_ref, cd_count_ref, mask):
    own, piece = lax.axis_index("owner"), lax.axis_index("blk")
    chunk = piece % (NZ * NC)
    z, x, core = own // (NX * NC), (own // NC) % NX, own % NC
    tasks, list_len = ab_ref.shape
    place = lax.broadcasted_iota(jnp.int32, (tasks, list_len), 1)
    task = lax.broadcasted_iota(jnp.int32, (tasks, tasks), 0)
    same = task == lax.broadcasted_iota(jnp.int32, (tasks, tasks), 1)

    def live(list_ref, count_ref):
        counts = jnp.where(same, count_ref[...].astype(jnp.float32), 0.0)
        counts = jnp.sum(counts, axis=1, keepdims=True)
        return jnp.where(place.astype(jnp.float32) < counts, list_ref[...], -1)

    ab_list, cd_list = live(ab_ref, ab_count_ref), live(cd_ref, cd_count_ref)
    group = lane_group((tasks, LANE), LANE // NX)

    def hit(tile_list, tile):
        return jnp.max((tile_list == tile).astype(jnp.float32), axis=1, keepdims=True)

    def ab_hit(low):
        mine, theirs = (hit(ab_list, owner_index(z, spot, core) * 2 + low) for spot in (x, x ^ 3))
        return jnp.where(group < 2, mine, theirs)

    def cd_hit(par):
        mine, theirs = (
            hit(cd_list, owner_index(chunk // NC, spot, chunk % NC) * 2 + par) for spot in (x, x ^ 1)
        )
        return jnp.where(group % 2 == 0, mine, theirs)

    cd_hits = [cd_hit(par) for par in range(2)]
    for low in range(2):
        rows_hit = ab_hit(low)
        for par in range(2):
            mask[low * 2 + par] = rows_hit * cd_hits[par]


def accumulate(mask, rows_ref, out_ref):
    totals = [jnp.zeros((SUB, LANE), jnp.float32) for _ in range(4)]
    for task in range(rows_ref.shape[0]):
        rows = rows_ref[task].astype(jnp.float32)
        for kind in range(4):
            totals[kind] += rows * mask[kind, task : task + 1, :]
    for kind in range(4):
        rounded = totals[kind].astype(out_ref.dtype)
        for target in range(out_ref.shape[0]):
            out_ref[target, kind] = rounded


def collect_near(*refs):
    own_ref, first_ref, second_ref, _ = refs[:4]
    near_ref, relay_ref, mask = refs[8:]
    make_masks(*refs[4:8], mask)
    for place, ref in enumerate((own_ref, first_ref, second_ref)):
        near_ref[place] = ref[...]
    relay_ref[...] = first_ref[...]


def settle(*refs):
    pass


def collect_rest(near_pair_ref, far_ref, far_pair_ref, _, out_ref):
    out_ref[: NZ - 1] = near_pair_ref[...]
    out_ref[NZ - 1] = far_ref[...]
    out_ref[NZ] = far_pair_ref[...]


def multiply(weights_ref, *rest):
    mine_ref, theirs_ref, left = rest[4:]
    amps = [((near, more, NZ - 1), (more, more, NZ)) for near, more in (rest[:2], rest[2:4])]
    own = lax.axis_index("owner")
    z, core = own // (NX * NC), own % NC
    width, occ = rest[0].shape[2:]
    chunks = NZ * NC
    blocks = [(par, d, side) for par in range(2) for d in range(2) for side in range(NC)]
    for kind in range(4):
        low, par = kind // 2, kind % 2
        for side in range(NC):
            parts = []
            for part in range(width // SUB):
                tiles = []
                for step in STEPS:
                    chunk = (z ^ step) * NC + (core + side) % NC
                    tiles.append(weights_ref[part * chunks + chunk, kind].astype(jnp.float32))
                parts.append(regroup(tiles, width))
            for a in range(2):
                for d in range(2):
                    rows = jnp.concatenate([p[2 * a + d] for p in parts], axis=0)
                    row, col = (a * 2 + low) * width, blocks.index((par, d, side)) * LANE
                    left[row : row + width, col : col + LANE] = rows.astype(left.dtype)
    wide = 256
    for col in range(0, occ, wide):
        total = None
        for at, (par, d, side) in enumerate(blocks):
            near, far, last = amps[side][d]
            right = [ref[place, par, :, col : col + wide] for ref, place in ((near, 0), (near, 1), (near, 2), (far, last))]
            right = jnp.concatenate(right, axis=0)
            term = jnp.dot(left[:, at * LANE : (at + 1) * LANE], right, preferred_element_type=jnp.float32)
            total = term if total is None else total + term
        mine_ref[:, col : col + wide] = total[: 2 * width]
        theirs_ref[:, col : col + wide] = total[2 * width :].astype(theirs_ref.dtype)


def moved(block, dz=0, dx=0, dcore=0):
    pairs = [
        (owner_index(z, x, core), owner_index(z ^ dz, x ^ dx, core ^ dcore))
        for z in range(NZ)
        for x in range(NX)
        for core in range(NC)
    ]
    return lax.ppermute(block, "owner", pairs)


def shards(amplitudes, integrals, cd_tiles, cd_count, ab_tiles, ab_count):
    tile_dev, width, occ = amplitudes.shape
    owners, pieces = lax.axis_size("owner"), lax.axis_size("blk")
    tasks = cd_tiles.shape[0]
    bf16, f32 = jnp.bfloat16, jnp.float32

    first, second = moved(amplitudes, 1), moved(amplitudes, 3)
    ordered = pl.pallas_call(
        order_columns,
        out_shape=jax.ShapeDtypeStruct((width // SUB, NZ * NC, SUB, LANE), bf16),
        in_specs=[SMEM, SMEM, VMEM],
        out_specs=VMEM,
        scratch_shapes=[pltpu.SMEM((owners,), jnp.int32)],
        name="order_columns",
    )(cd_tiles, cd_count, integrals[0])
    ordered = ordered.reshape(pieces, SUB, LANE)
    mine = lax.all_to_all(ordered, "blk", split_axis=0, concat_axis=0, tiled=True)
    outgoing = pl.pallas_call(
        route,
        out_shape=jax.ShapeDtypeStruct((owners, SUB, LANE), bf16),
        in_specs=[SMEM, SMEM, VMEM],
        out_specs=VMEM,
        scratch_shapes=[pltpu.SMEM((owners,), jnp.int32)],
        compiler_params=SMALL,
        name="route",
    )(ab_tiles, ab_count, mine)
    near, relay, mask = pl.pallas_call(
        collect_near,
        out_shape=(
            jax.ShapeDtypeStruct((NZ - 1, tile_dev, width, occ), bf16),
            jax.ShapeDtypeStruct(second.shape, bf16),
            jax.ShapeDtypeStruct((4, tasks, LANE), f32),
        ),
        in_specs=[VMEM] * 3 + [ANY] + [VMEM] * 4,
        out_specs=(VMEM, VMEM, VMEM),
        cost_estimate=pl.CostEstimate(flops=10000000000, bytes_accessed=amplitudes.size * 16, transcendentals=0),
        compiler_params=SMALL,
        name="collect_near",
    )(amplitudes, first, second, mine, ab_tiles, ab_count[None, :], cd_tiles, cd_count[None, :])
    near_pair = moved(near, dx=1)
    near_other = moved(near, dcore=1)
    far = moved(relay, 3)
    arrived = lax.all_to_all(outgoing, "owner", split_axis=0, concat_axis=0, tiled=True)
    spread = pl.pallas_call(
        accumulate,
        out_shape=jax.ShapeDtypeStruct((pieces, 4, SUB, LANE), bf16),
        in_specs=[VMEM] * 2,
        out_specs=VMEM,
        compiler_params=SMALL,
        name="accumulate",
    )(mask, arrived)
    far = pl.pallas_call(
        settle,
        out_shape=jax.ShapeDtypeStruct(far.shape, far.dtype),
        in_specs=[ANY, ANY],
        out_specs=ANY,
        input_output_aliases={0: 0},
        cost_estimate=pl.CostEstimate(flops=2000000000, bytes_accessed=far.size * 4, transcendentals=0),
        compiler_params=SMALL,
        name="settle",
    )(far, spread)
    far_pair = moved(far, dx=1)
    rest = pl.pallas_call(
        collect_rest,
        out_shape=jax.ShapeDtypeStruct((NZ + 1, tile_dev, width, occ), bf16),
        in_specs=[VMEM] * 3 + [ANY],
        out_specs=VMEM,
        cost_estimate=pl.CostEstimate(flops=2000000000, bytes_accessed=amplitudes.size * 20, transcendentals=0),
        compiler_params=SMALL,
        name="collect_rest",
    )(near_pair, far, far_pair, near_other)
    sides = [near, rest, near_other, moved(rest, dcore=1)]

    weights = lax.all_to_all(spread, "blk", split_axis=0, concat_axis=0, tiled=True)
    shape = (tile_dev * width, occ)
    mine, theirs = pl.pallas_call(
        multiply,
        out_shape=(jax.ShapeDtypeStruct(shape, f32), jax.ShapeDtypeStruct(shape, bf16)),
        in_specs=[VMEM] * 5,
        out_specs=(VMEM, VMEM),
        scratch_shapes=[pltpu.VMEM((2 * tile_dev * width, 2 * NZ * NC * tile_dev * width), bf16)],
        compiler_params=pltpu.CompilerParams(vmem_limit_bytes=16 * 1024 * 1024),
        name="multiply",
    )(weights, *sides)
    return (mine + moved(theirs, dx=3).astype(f32)).reshape(tile_dev, width, occ)


def solution(mesh):
    placed = (P("owner", None, "blk"), P("owner", "blk", None), P(), P(), P(), P())
    return jax.shard_map(
        shards, mesh=mesh, in_specs=placed, out_specs=P("owner", None, "blk"), check_vma=False
    )
```

```python
import functools

import jax
import jax.numpy as jnp
from jax import lax
from jax.experimental import pallas as pl
from jax.experimental.pallas import tpu as pltpu
from jax.sharding import PartitionSpec as P

NZ, NX, NC = 4, 4, 2
SUB, LANE = 8, 128
SMEM = pl.BlockSpec(memory_space=pltpu.SMEM)
VMEM = pl.BlockSpec(memory_space=pltpu.VMEM)
ANY = pl.BlockSpec(memory_space=pl.ANY)
SMALL = pltpu.CompilerParams(vmem_limit_bytes=4 * 1024 * 1024)
STEPS = (0, 1, 3, 2)


def owner_index(z, x, core):
    return (z * NX + x) * NC + core


def lane_group(shape, width):
    return lax.broadcasted_iota(jnp.int32, shape, len(shape) - 1) // width


def invert(tiles_ref, count_ref, where_ref):
    own = lax.axis_index("owner")
    for owner in range(where_ref.shape[0]):
        where_ref[owner] = -1
    count = count_ref[own]
    for place in range(tiles_ref.shape[1]):
        owner = tiles_ref[own, place] // 2

        @pl.when(place < count)
        def _():
            where_ref[owner] = place


def order_columns(tiles_ref, count_ref, rows_ref, out_ref, where_ref):
    width = rows_ref.shape[0]
    groups = LANE // width
    invert(tiles_ref, count_ref, where_ref)
    group = lane_group((width, LANE), width)
    for z in range(NZ):
        for core in range(NC):
            merged = jnp.zeros((width, LANE), jnp.float32)
            for spot in range(NX):
                found = where_ref[owner_index(z, spot, core)]
                place = jnp.maximum(found, 0)
                start = pl.multiple_of(place // groups * LANE, LANE)
                chunk = rows_ref[:, pl.ds(start, LANE)].astype(jnp.float32)
                turned = pltpu.roll(chunk, (spot - place % groups + groups) % groups * width, 1)
                merged = jnp.where((group == spot) & (found >= 0), turned, merged)
            for part in range(width // SUB):
                out_ref[part, z * NC + core] = merged[part * SUB : (part + 1) * SUB].astype(out_ref.dtype)


def regroup(tiles, width):
    count = len(tiles)
    group = lane_group(tiles[0].shape, width)
    results = []
    for i in range(count):
        merged = None
        for j in range(count):
            shift = (j - i) % count * width
            turned = pltpu.roll(tiles[j], shift, tiles[j].ndim - 1) if shift else tiles[j]
            merged = turned if merged is None else jnp.where(group == j, turned, merged)
        results.append(merged)
    return results


def route(tiles_ref, count_ref, rows_ref, out_ref, where_ref):
    invert(tiles_ref, count_ref, where_ref)

    def held(owner):
        found = where_ref[owner]
        return jnp.where(found >= 0, rows_ref[jnp.maximum(found, 0)].astype(jnp.float32), 0.0)

    width = LANE // NX
    group = lane_group((SUB, LANE), width)
    for z in range(NZ):
        for core in range(NC):
            tiles = [held(owner_index(z, x, core)) for x in range(NX)]
            for x in range(NX):
                wanted = [(tiles[x ^ (3 * a)], x ^ d) for a in range(2) for d in range(2)]
                merged = None
                for place, (tile, spot) in enumerate(wanted):
                    shift = (place - spot) % NX * width
                    turned = pltpu.roll(tile, shift, 1) if shift else tile
                    merged = turned if merged is None else jnp.where(group == place, turned, merged)
                out_ref[owner_index(z, x, core)] = merged.astype(out_ref.dtype)


def make_masks(ab_ref, ab_count_ref, cd_ref, cd_count_ref, mask):
    own, piece = lax.axis_index("owner"), lax.axis_index("blk")
    chunk = piece % (NZ * NC)
    z, x, core = own // (NX * NC), (own // NC) % NX, own % NC
    tasks, list_len = ab_ref.shape
    place = lax.broadcasted_iota(jnp.int32, (tasks, list_len), 1)
    task = lax.broadcasted_iota(jnp.int32, (tasks, tasks), 0)
    same = task == lax.broadcasted_iota(jnp.int32, (tasks, tasks), 1)

    def live(list_ref, count_ref):
        counts = jnp.where(same, count_ref[...].astype(jnp.float32), 0.0)
        counts = jnp.sum(counts, axis=1, keepdims=True)
        return jnp.where(place.astype(jnp.float32) < counts, list_ref[...], -1)

    ab_list, cd_list = live(ab_ref, ab_count_ref), live(cd_ref, cd_count_ref)
    group = lane_group((tasks, LANE), LANE // NX)

    def hit(tile_list, tile):
        return jnp.max((tile_list == tile).astype(jnp.float32), axis=1, keepdims=True)

    def ab_hit(low):
        mine, theirs = (hit(ab_list, owner_index(z, spot, core) * 2 + low) for spot in (x, x ^ 3))
        return jnp.where(group < 2, mine, theirs)

    def cd_hit(par):
        mine, theirs = (
            hit(cd_list, owner_index(chunk // NC, spot, chunk % NC) * 2 + par) for spot in (x, x ^ 1)
        )
        return jnp.where(group % 2 == 0, mine, theirs)

    cd_hits = [cd_hit(par) for par in range(2)]
    for low in range(2):
        rows_hit = ab_hit(low)
        for par in range(2):
            mask[low * 2 + par] = rows_hit * cd_hits[par]


def accumulate(mask, rows_ref, out_ref):
    totals = [jnp.zeros((SUB, LANE), jnp.float32) for _ in range(4)]
    for task in range(rows_ref.shape[0]):
        rows = rows_ref[task].astype(jnp.float32)
        for kind in range(4):
            totals[kind] += rows * mask[kind, task : task + 1, :]
    for kind in range(4):
        rounded = totals[kind].astype(out_ref.dtype)
        for target in range(out_ref.shape[0]):
            out_ref[target, kind] = rounded


def collect_near(*refs):
    own_ref, first_ref, second_ref, _ = refs[:4]
    near_ref, relay_ref, mask = refs[8:]
    make_masks(*refs[4:8], mask)
    for place, ref in enumerate((own_ref, first_ref, second_ref)):
        near_ref[place] = ref[...]
    relay_ref[...] = first_ref[...]


def settle(*refs):
    pass


def collect_rest(near_pair_ref, far_ref, _, out_ref):
    out_ref[: NZ - 1] = near_pair_ref[...]
    out_ref[NZ - 1] = far_ref[...]


def multiply(weights_ref, *rest):
    mine_ref, theirs_ref, left = rest[6:]
    amps = [((near, more.at[NZ - 1]), (more, last)) for near, more, last in (rest[:3], rest[3:6])]
    own = lax.axis_index("owner")
    z, core = own // (NX * NC), own % NC
    width, occ = rest[0].shape[2:]
    chunks = NZ * NC
    blocks = [(par, d, side) for par in range(2) for d in range(2) for side in range(NC)]
    for kind in range(4):
        low, par = kind // 2, kind % 2
        for side in range(NC):
            parts = []
            for part in range(width // SUB):
                tiles = []
                for step in STEPS:
                    chunk = (z ^ step) * NC + (core + side) % NC
                    tiles.append(weights_ref[part * chunks + chunk, kind].astype(jnp.float32))
                parts.append(regroup(tiles, width))
            for a in range(2):
                for d in range(2):
                    rows = jnp.concatenate([p[2 * a + d] for p in parts], axis=0)
                    row, col = (a * 2 + low) * width, blocks.index((par, d, side)) * LANE
                    left[row : row + width, col : col + LANE] = rows.astype(left.dtype)
    wide = 256
    for col in range(0, occ, wide):
        total = None
        for at, (par, d, side) in enumerate(blocks):
            near, far = amps[side][d]
            right = [near[place, par, :, col : col + wide] for place in range(NZ - 1)]
            right.append(far[par, :, col : col + wide])
            right = jnp.concatenate(right, axis=0)
            term = jnp.dot(left[:, at * LANE : (at + 1) * LANE], right, preferred_element_type=jnp.float32)
            total = term if total is None else total + term
        mine_ref[:, col : col + wide] = total[: 2 * width]
        theirs_ref[:, col : col + wide] = total[2 * width :].astype(theirs_ref.dtype)


def moved(block, dz=0, dx=0, dcore=0):
    pairs = [
        (owner_index(z, x, core), owner_index(z ^ dz, x ^ dx, core ^ dcore))
        for z in range(NZ)
        for x in range(NX)
        for core in range(NC)
    ]
    return lax.ppermute(block, "owner", pairs)


def shards(amplitudes, integrals, cd_tiles, cd_count, ab_tiles, ab_count):
    tile_dev, width, occ = amplitudes.shape
    owners, pieces = lax.axis_size("owner"), lax.axis_size("blk")
    tasks = cd_tiles.shape[0]
    bf16, f32 = jnp.bfloat16, jnp.float32

    first, second = moved(amplitudes, 1), moved(amplitudes, 3)
    ordered = pl.pallas_call(
        order_columns,
        out_shape=jax.ShapeDtypeStruct((width // SUB, NZ * NC, SUB, LANE), bf16),
        in_specs=[SMEM, SMEM, VMEM],
        out_specs=VMEM,
        scratch_shapes=[pltpu.SMEM((owners,), jnp.int32)],
        name="order_columns",
    )(cd_tiles, cd_count, integrals[0])
    ordered = ordered.reshape(pieces, SUB, LANE)
    mine = lax.all_to_all(ordered, "blk", split_axis=0, concat_axis=0, tiled=True)
    outgoing = pl.pallas_call(
        route,
        out_shape=jax.ShapeDtypeStruct((owners, SUB, LANE), bf16),
        in_specs=[SMEM, SMEM, VMEM],
        out_specs=VMEM,
        scratch_shapes=[pltpu.SMEM((owners,), jnp.int32)],
        compiler_params=SMALL,
        name="route",
    )(ab_tiles, ab_count, mine)
    near, relay, mask = pl.pallas_call(
        collect_near,
        out_shape=(
            jax.ShapeDtypeStruct((NZ - 1, tile_dev, width, occ), bf16),
            jax.ShapeDtypeStruct(second.shape, bf16),
            jax.ShapeDtypeStruct((4, tasks, LANE), f32),
        ),
        in_specs=[VMEM] * 3 + [ANY] + [VMEM] * 4,
        out_specs=(VMEM, VMEM, VMEM),
        cost_estimate=pl.CostEstimate(flops=10000000000, bytes_accessed=amplitudes.size * 16, transcendentals=0),
        compiler_params=SMALL,
        name="collect_near",
    )(amplitudes, first, second, mine, ab_tiles, ab_count[None, :], cd_tiles, cd_count[None, :])
    near_pair = moved(near, dx=1)
    near_other = moved(near, dcore=1)
    far = moved(relay, 3)
    arrived = lax.all_to_all(outgoing, "owner", split_axis=0, concat_axis=0, tiled=True)
    spread = pl.pallas_call(
        accumulate,
        out_shape=jax.ShapeDtypeStruct((pieces, 4, SUB, LANE), bf16),
        in_specs=[VMEM] * 2,
        out_specs=VMEM,
        compiler_params=SMALL,
        name="accumulate",
    )(mask, arrived)
    far = pl.pallas_call(
        settle,
        out_shape=jax.ShapeDtypeStruct(far.shape, far.dtype),
        in_specs=[ANY, ANY],
        out_specs=ANY,
        input_output_aliases={0: 0},
        cost_estimate=pl.CostEstimate(flops=2000000000, bytes_accessed=far.size * 4, transcendentals=0),
        compiler_params=SMALL,
        name="settle",
    )(far, spread)
    far_pair = moved(far, dx=1)
    rest = pl.pallas_call(
        collect_rest,
        out_shape=jax.ShapeDtypeStruct((NZ, tile_dev, width, occ), bf16),
        in_specs=[VMEM] * 2 + [ANY],
        out_specs=VMEM,
        cost_estimate=pl.CostEstimate(flops=2000000000, bytes_accessed=amplitudes.size * 20, transcendentals=0),
        compiler_params=SMALL,
        name="collect_rest",
    )(near_pair, far, near_other)
    sides = [near, rest, far_pair, near_other, moved(rest, dcore=1), moved(far_pair, dcore=1)]

    weights = lax.all_to_all(spread, "blk", split_axis=0, concat_axis=0, tiled=True)
    shape = (tile_dev * width, occ)
    mine, theirs = pl.pallas_call(
        multiply,
        out_shape=(jax.ShapeDtypeStruct(shape, f32), jax.ShapeDtypeStruct(shape, bf16)),
        in_specs=[VMEM] * 7,
        out_specs=(VMEM, VMEM),
        scratch_shapes=[pltpu.VMEM((2 * tile_dev * width, 2 * NZ * NC * tile_dev * width), bf16)],
        compiler_params=pltpu.CompilerParams(vmem_limit_bytes=16 * 1024 * 1024),
        name="multiply",
    )(weights, *sides)
    return (mine + moved(theirs, dx=3).astype(f32)).reshape(tile_dev, width, occ)


def solution(mesh):
    placed = (P("owner", None, "blk"), P("owner", "blk", None), P(), P(), P(), P())
    return jax.shard_map(
        shards, mesh=mesh, in_specs=placed, out_specs=P("owner", None, "blk"), check_vma=False
    )
```
